512 devices in a mesh: lat: 16 (over z), lon: 32 (over y, x, core).
Axes of the slice: x: 4, y: 4, z: 16, core: 2. Of those that a mesh axis runs over, the one named last changes fastest.
Arguments:
- state: float32 [4, 32, 256, 4096], P(None, None, 'lat', 'lon'), may hold values from -6 to 6
- damping: float32 [32], replicated, may hold values from 0.02 to 0.2
- cutoff: int32 [256], replicated, may hold values from 1 to 2048, as said below
Outputs:
- advanced: float32 [4, 32, 256, 4096], P(None, None, 'lat', 'lon')
The draws below stay inside these ranges and needn't reach their ends.
Inputs may be any that keep to these rules, and one draw needn't show every extreme that they name: cutoff[j] is 2048 on every row within 45 degrees of the equator and 1 on the two outermost rows.
All inputs are finite; a program needn't handle non-finite values.
Results may differ from the reference program's by a relative error of at most 0.00005.
Values sent between devices are 32-bit elements; how exact they have to be, the bound alone decides.
No kernel may reach another device: no remote copies, remote signals or barrier semaphores. Data moves between devices by JAX's collectives and lax.ppermute only.
A program may use at most 64 MiB of HBM per device.

```python
import math
import jax
import jax.numpy as jnp
import numpy as np
from jax import lax

NLON = 4096
LEV = 32
NLAT = 256


def draw_cutoff(key, part):
    key = jax.random.fold_in(key, 11)
    rows_np = np.arange(NLAT)
    phi_np = math.pi * ((rows_np + 0.5) / NLAT - 0.5)
    base_np = np.floor(NLON // 2 * np.cos(phi_np) / math.cos(math.pi / 4) + 0.5)
    base_np = np.clip(base_np, 1, NLON // 2).astype(np.int32)
    base = jnp.asarray(base_np, dtype=jnp.int32)
    rows = jnp.arange(NLAT, dtype=jnp.int32)
    from_pole = jnp.minimum(rows, NLAT - 1 - rows)
    quarter = NLAT // 4
    bits = jax.random.randint(key, (NLAT,), 0, 1 << 30)
    jitter = bits % (base // 4 + 1)
    value = jnp.maximum(base - jitter, 1)
    value = jnp.where(from_pole >= quarter, NLON // 2, value)
    return jnp.where(from_pole == 0, 1, value).astype(jnp.int32)


def steps_of(key, shape, pieces, smallest, top_value):
    factor_of, own = 1.0, jax.random.fold_in(key, 6)
    for axis_at, blocks in pieces:
        heights = jnp.exp(jax.random.uniform(jax.random.fold_in(own, axis_at), (blocks,), jnp.float32, smallest / len(pieces), top_value / len(pieces)))
        factor_of = factor_of * jnp.repeat(heights, shape[axis_at] // blocks).reshape([-1 if axis == axis_at else 1 for axis in range(len(shape))])
    return factor_of


def centred(rng, extent, spread, limit, cuts=(), kind=jnp.bfloat16):
    loudness = steps_of(rng, extent, cuts, -0.22, 0.18) if cuts else 1.0
    values = jax.random.normal(rng, extent, jnp.float32) * spread * loudness
    return jnp.minimum(jnp.maximum(values, -limit), limit).astype(kind)


def setup_inputs(seed: int = 0) -> dict:
    key_of = jax.random.split(jax.random.key(seed), 4)
    state = centred(key_of[0], (4, LEV, NLAT, NLON), 1.0, 6.0, ((2, 16), (3, 32)), jnp.float32)
    damping = jnp.clip(jnp.exp(jax.random.uniform(key_of[1], (LEV,), jnp.float32, math.log(0.02), math.log(0.2))), 0.02, 0.2)
    cutoff = draw_cutoff(jax.random.fold_in(key_of[3], 71), 0)
    return {"state": state, "damping": damping, "cutoff": cutoff}


COURANT = 0.05


def metrics(rows, nlat):
    angle = math.pi * ((rows.astype(jnp.float32) + 0.5) / nlat - 0.5)
    return jnp.cos(angle), 2.0 * jnp.sin(angle)


def reference(state, damping, cutoff):
    rows = jnp.arange(NLAT)
    cosine, coriolis = metrics(rows, NLAT)
    cos_north, unused_north = metrics(rows + 1, NLAT)
    cos_south, unused_south = metrics(rows - 1, NLAT)
    cosine = cosine[:, None]
    coriolis = coriolis[:, None]
    cos_north = cos_north[:, None]
    cos_south = cos_south[:, None]
    polar = (rows < NLAT // 4) | (rows >= NLAT - NLAT // 4)
    waves = jnp.arange(NLON // 2 + 1)
    keep = waves[None, :] <= cutoff[:, None]

    def north(field):
        return jnp.concatenate([field[1:], jnp.zeros_like(field[:1])], 0)

    def south(field):
        return jnp.concatenate([jnp.zeros_like(field[:1]), field[:-1]], 0)

    def zonal_diff(field):
        return (jnp.roll(field, -1, 1) - jnp.roll(field, 1, 1)) / (2.0 * cosine)

    def merid_flux(field):
        return (cos_north * north(field) - cos_south * south(field)) / (2.0 * cosine)

    def merid_diff(field):
        return (north(field) - south(field)) * 0.5

    def level_step(inputs):
        fields, damp_scale = inputs
        thick, zonal, merid, potential = fields[0], fields[1], fields[2], fields[3]
        divergence = zonal_diff(zonal) + merid_flux(merid)
        carried = 1.0 + thick
        inc_thick = -COURANT * (zonal_diff(carried * zonal) + merid_flux(carried * merid))
        damp_rows = damp_scale * cosine * cosine
        inc_zonal = COURANT * (coriolis * merid - zonal_diff(thick)) + damp_rows * zonal_diff(divergence)
        inc_merid = COURANT * (-coriolis * zonal - merid_diff(thick)) + damp_rows * merid_diff(divergence)
        inc_pot = -COURANT * (zonal * zonal_diff(potential) + merid * merid_diff(potential))
        increment = jnp.stack([inc_thick, inc_zonal, inc_merid, inc_pot], 0)
        spectrum = jnp.fft.rfft(increment, axis=-1)
        smooth = jnp.fft.irfft(spectrum * keep[None], n=NLON, axis=-1).astype(increment.dtype)
        increment = jnp.where(polar[None, :, None], smooth, increment)
        return fields + increment

    moved = jnp.moveaxis(state, 1, 0)
    result = lax.map(level_step, (moved, damping))
    return jnp.moveaxis(result, 0, 1)
```

```python
import math

import jax
import jax.numpy as jnp
import numpy as np
from jax import lax
from jax.experimental import pallas as pl
from jax.experimental.pallas import tpu as pltpu
from jax.sharding import PartitionSpec as P

COURANT = 0.05
ROWS = 8
LANES = 128


def metrics(rows, nlat):
    angle = math.pi * ((rows.astype(jnp.float32) + 0.5) / nlat - 0.5)
    return jnp.cos(angle), 2.0 * jnp.sin(angle)


def row_tables(first, nlat, damping, cutoff):
    rows = first - 1 + jnp.arange(ROWS + 2)
    cosine, coriolis = metrics(rows, nlat)
    cos_north = metrics(rows + 1, nlat)[0]
    cos_south = metrics(rows - 1, nlat)[0]
    half = 0.5 / cosine
    inside = ((rows >= 0) & (rows < nlat)).astype(jnp.float32)
    own = [
        half,
        cos_north * half,
        cos_south * half,
        coriolis,
        damping[0] * cosine * cosine,
        damping[1] * cosine * cosine,
    ]
    tiles = [jnp.broadcast_to(v[1:-1, None], (ROWS, LANES)) for v in own]
    for at in (0, ROWS + 1):
        for v in (half, cos_north * half, cos_south * half, jnp.ones_like(half)):
            tiles.append(jnp.broadcast_to((v * inside)[at], (ROWS, LANES)))
    rows = rows[1:-1]
    polar = (rows < nlat // 4) | (rows >= nlat - nlat // 4)
    limit = lax.dynamic_slice(cutoff, (first,), (ROWS,))
    limits = [jnp.broadcast_to(v[:, None], (ROWS, LANES)) for v in (limit, polar.astype(jnp.int32))]
    return jnp.stack(tiles), jnp.stack(limits)


def split(values):
    high = values.astype(jnp.bfloat16)
    low = (values - high.astype(jnp.float32)).astype(jnp.bfloat16)
    return high, low


def fourier_tables(blocks):
    nlon = blocks * LANES
    at = np.arange(LANES)
    phase = 2.0 * np.pi * ((at[:, None] * at[None, :]) % LANES) / LANES
    cos, sin = np.cos(phase), np.sin(phase)
    forward = np.block([[cos, -sin], [sin, cos]])
    inverse = np.block([[cos, sin], [-sin, cos]]) / nlon
    turn = 2.0 * np.pi * np.arange(blocks // 2 + 1)[:, None] * at[None, :] / nlon
    twist = np.stack([np.cos(turn), np.sin(turn)]).astype(np.float32)
    twist = np.broadcast_to(twist[:, :, None, :], (2, blocks // 2 + 1, ROWS, LANES))

    def halves(matrix):
        high = matrix.astype(np.float32).astype(jnp.bfloat16)
        low = (matrix - high.astype(np.float64)).astype(np.float32).astype(jnp.bfloat16)
        return np.stack([high, low])

    return np.ascontiguousarray(twist), halves(forward), halves(inverse)


def root(k, n):
    angle = 2.0 * math.pi * k / n
    return math.cos(angle), math.sin(angle)


def real_fft(x):
    n = len(x)
    if n == 2:
        return [(x[0] + x[1], None), (x[0] - x[1], None)]
    even, odd = real_fft(x[0::2]), real_fft(x[1::2])
    half, quarter = n // 2, n // 4
    out = [None] * (half + 1)
    out[0] = (even[0][0] + odd[0][0], None)
    out[half] = (even[0][0] - odd[0][0], None)
    out[quarter] = (even[quarter][0], -odd[quarter][0])
    for k in range(1, quarter):
        c, s = root(k, n)
        re, im = odd[k]
        t_re, t_im = re * c + im * s, im * c - re * s
        out[k] = (even[k][0] + t_re, even[k][1] + t_im)
        out[half - k] = (even[k][0] - t_re, t_im - even[k][1])
    return out


def real_ifft(w):
    half = len(w) - 1
    n, quarter = 2 * half, half // 2
    if n == 2:
        return [w[0][0] + w[1][0], w[0][0] - w[1][0]]
    even, odd = [None] * (quarter + 1), [None] * (quarter + 1)
    even[0] = (w[0][0] + w[half][0], None)
    odd[0] = (w[0][0] - w[half][0], None)
    even[quarter] = (2.0 * w[quarter][0], None)
    odd[quarter] = (-2.0 * w[quarter][1], None)
    for k in range(1, quarter):
        c, s = root(k, n)
        a, b = w[k], w[half - k]
        even[k] = (a[0] + b[0], a[1] - b[1])
        re, im = a[0] - b[0], a[1] + b[1]
        odd[k] = (re * c - im * s, im * c + re * s)
    x = [None] * n
    x[0::2], x[1::2] = real_ifft(even), real_ifft(odd)
    return x


def pack_kernel(blocks, x_ref, z_ref, c_ref, own_ref):
    core = lax.axis_index("lon") % 2
    stride = 8 * ROWS

    def plane(field, level, row):
        return x_ref[pl.ds((field * 2 + level) * ROWS + row, blocks, stride=stride), :]

    for out, end in ((z_ref, core), (c_ref, 1 - core)):
        edge, inner = end * (ROWS - 1), 1 + end * (ROWS - 3)
        for k, (field, row) in enumerate(((0, edge), (1, edge), (3, edge), (2, edge), (2, inner))):
            for level in range(2):
                out[k * 2 + level] = plane(field, level, row)
    for side in range(2):
        for level in range(2):
            own_ref[side * 2 + level] = plane(2, level, side * (ROWS - 1))


def main_kernel(
    blocks,
    x_ref,
    z_ref,
    c_ref,
    own_ref,
    tab_ref,
    limit_ref,
    twist_ref,
    forward_ref,
    inverse_ref,
    out_ref,
    inc_ref,
    div_ref,
    edge_ref,
    wave_ref,
):
    core = lax.axis_index("lon") % 2
    lane = lax.broadcasted_iota(jnp.int32, (ROWS, LANES), 1)
    row = lax.broadcasted_iota(jnp.int32, (ROWS, LANES), 0)
    first_lane, last_lane = lane == 0, lane == LANES - 1
    first_row, last_row = row == 0, row == ROWS - 1

    def east(here, after):
        return pltpu.roll(jnp.where(first_lane, after, here), LANES - 1, axis=1)

    def west(here, before):
        return pltpu.roll(jnp.where(last_lane, before, here), 1, axis=1)

    def north(here, beyond):
        return jnp.where(last_row, beyond, pltpu.roll(here, ROWS - 1, axis=0))

    def south(here, beyond):
        return jnp.where(first_row, beyond, pltpu.roll(here, 1, axis=0))

    wide = lax.broadcasted_iota(jnp.int32, (blocks, LANES), 1)
    for side in range(2):
        from_z = core == side
        half, up, down, inside = (tab_ref[6 + side * 4 + i][:1] for i in range(4))
        for level in range(2):

            def beyond(k):
                other = c_ref[1 - core, k * 2 + level]
                return jnp.where(from_z, z_ref[k * 2 + level], other) * inside

            thick, zonal, potential, near, far = (beyond(k) for k in range(5))
            after = pltpu.roll(zonal, blocks - 1, axis=0)
            before = pltpu.roll(zonal, 1, axis=0)
            after = pltpu.roll(jnp.where(wide == 0, after, zonal), LANES - 1, axis=1)
            before = pltpu.roll(jnp.where(wide == LANES - 1, before, zonal), 1, axis=1)
            own = own_ref[side * 2 + level]
            above, below = (far, own) if side else (own, far)
            div = (after - before) * half + up * above - down * below
            for k, v in enumerate(((1.0 + thick) * near, near, thick, potential, div)):
                edge_ref[side, k * 2 + level] = v

    half, up, down, coriolis = (tab_ref[i] for i in range(4))

    def ends(k, level, p):
        return edge_ref[0, k * 2 + level, pl.ds(p, 1), :], edge_ref[1, k * 2 + level, pl.ds(p, 1), :]

    def divergence(p, carry):
        before, after = lax.rem(p + blocks - 1, blocks), lax.rem(p + 1, blocks)
        for level in range(2):
            u, v = 2 + level, 4 + level
            zonal, merid = x_ref[p, u], x_ref[p, v]
            lo, hi = ends(1, level, p)
            div_ref[p, level] = (
                (east(zonal, x_ref[after, u]) - west(zonal, x_ref[before, u])) * half
                + up * north(merid, hi)
                - down * south(merid, lo)
            )
        return carry

    lax.fori_loop(0, blocks, divergence, 0, unroll=4)

    def increments(p, carry):
        before, after = lax.rem(p + blocks - 1, blocks), lax.rem(p + 1, blocks)
        for level in range(2):
            h, u, v, t = level, 2 + level, 4 + level, 6 + level
            damp = tab_ref[4 + level]
            thick, zonal, merid, potential = x_ref[p, h], x_ref[p, u], x_ref[p, v], x_ref[p, t]
            thick_b, thick_a = x_ref[before, h], x_ref[after, h]
            carried = 1.0 + thick
            flux = carried * zonal
            flux_a = (1.0 + thick_a) * x_ref[after, u]
            flux_b = (1.0 + thick_b) * x_ref[before, u]
            flow = carried * merid
            lo, hi = ends(0, level, p)
            inc_ref[p, h] = -COURANT * (
                (east(flux, flux_a) - west(flux, flux_b)) * half
                + up * north(flow, hi)
                - down * south(flow, lo)
            )
            div = div_ref[p, level]
            slope = (east(thick, thick_a) - west(thick, thick_b)) * half
            spread = (east(div, div_ref[after, level]) - west(div, div_ref[before, level])) * half
            inc_ref[p, u] = COURANT * (coriolis * merid - slope) + damp * spread
            lo, hi = ends(2, level, p)
            slope = (north(thick, hi) - south(thick, lo)) * 0.5
            lo, hi = ends(4, level, p)
            spread = (north(div, hi) - south(div, lo)) * 0.5
            inc_ref[p, v] = COURANT * (-coriolis * zonal - slope) + damp * spread
            slope = (east(potential, x_ref[after, t]) - west(potential, x_ref[before, t])) * half
            lo, hi = ends(3, level, p)
            rise = (north(potential, hi) - south(potential, lo)) * 0.5
            inc_ref[p, t] = -COURANT * (zonal * slope + merid * rise)
        return carry

    lax.fori_loop(0, blocks, increments, 0, unroll=2)

    polar = limit_ref[1]
    top = blocks // 2
    nlon = blocks * LANES

    @pl.when(jnp.max(polar) == 0)
    def _():
        out_ref[...] = x_ref[...] + inc_ref[...]

    @pl.when(jnp.max(polar) > 0)
    def _():
        def analyse(g, carry):
            waves = real_fft([inc_ref[p, g] for p in range(blocks)])
            rows = pl.ds(pl.multiple_of(g * ROWS, ROWS), ROWS)
            for k, (re, im) in enumerate(waves):
                c, s = twist_ref[0, k], twist_ref[1, k]
                if im is None:
                    turned = (re, jnp.zeros_like(re)) if k == 0 else (re * c, -(re * s))
                else:
                    turned = (re * c + im * s, im * c - re * s)
                wave_ref[k, rows, :LANES], wave_ref[k, rows, LANES:] = turned
            return carry

        lax.fori_loop(0, 8, analyse, 0)

        def product(values, table_ref):
            high, low = split(values)
            dot = lambda a, b: jnp.dot(a, b, preferred_element_type=jnp.float32)
            return dot(high, table_ref[0]) + dot(low, table_ref[0]) + dot(high, table_ref[1])

        count = (top + 1) * 8 * ROWS
        spectrum = product(wave_ref[...].reshape(count, 2 * LANES), forward_ref)
        spectrum = spectrum.reshape(top + 1, 8, ROWS, 2 * LANES)
        wave = lax.broadcasted_iota(jnp.int32, (top + 1, 1, ROWS, LANES), 0)
        wave = wave + blocks * lax.broadcasted_iota(jnp.int32, (top + 1, 1, ROWS, LANES), 3)
        kept = jnp.minimum(wave, nlon - wave) <= limit_ref[0]
        kept = jnp.concatenate([kept, kept], axis=-1)
        spectrum = jnp.where(kept, spectrum, 0.0).reshape(count, 2 * LANES)
        wave_ref[...] = product(spectrum, inverse_ref).reshape(top + 1, 8 * ROWS, 2 * LANES)

        def rebuild(g, carry):
            rows = pl.ds(pl.multiple_of(g * ROWS, ROWS), ROWS)
            waves = []
            for k in range(top + 1):
                re, im = wave_ref[k, rows, :LANES], wave_ref[k, rows, LANES:]
                c, s = twist_ref[0, k], twist_ref[1, k]
                if k == 0:
                    waves.append((re, None))
                elif k == top:
                    waves.append((re * c - im * s, None))
                else:
                    waves.append((re * c - im * s, im * c + re * s))
            for p, smooth in enumerate(real_ifft(waves)):
                out_ref[p, g] = x_ref[p, g] + jnp.where(polar > 0, smooth, inc_ref[p, g])
            return carry

        lax.fori_loop(0, 8, rebuild, 0)


def on_device(state, damping, cutoff):
    fields, levels, nrow, ncol = state.shape
    nlat = nrow * lax.axis_size("lat")
    blocks = lax.axis_size("lon")
    bands = lax.axis_size("lat")
    lat, lon = lax.axis_index("lat"), lax.axis_index("lon")
    core = lon % 2
    chips = blocks // 2

    parts = state.reshape(fields, chips, 2, 2, ROWS, ncol).transpose(1, 3, 0, 2, 4, 5)
    parts = parts.reshape(blocks, fields * 2, ROWS, ncol)
    circles = lax.all_to_all(parts, "lon", split_axis=0, concat_axis=0, tiled=True)

    first = lat * nrow + core * ROWS
    damp = lax.dynamic_slice(damping, (lon // 2 * 2,), (2,))
    tables, limits = row_tables(first, nlat, damp, cutoff)
    twist, forward, inverse = fourier_tables(blocks)

    vmem = pl.BlockSpec(memory_space=pltpu.VMEM)
    params = pltpu.CompilerParams(vmem_limit_bytes=40 * 2**20)
    plane = jax.ShapeDtypeStruct((10, blocks, ncol), jnp.float32)
    z_mine, c_mine, own = pl.pallas_call(
        lambda *refs: pack_kernel(blocks, *refs),
        out_shape=(plane, plane, jax.ShapeDtypeStruct((4, blocks, ncol), jnp.float32)),
        in_specs=[vmem],
        out_specs=(vmem, vmem, vmem),
        compiler_params=params,
        name="pack",
    )(circles.reshape(-1, ncol))

    swaps = []
    for z in range(bands):
        for m in range(chips):
            a, b = z * blocks + 2 * m + 1, (z + 1) % bands * blocks + 2 * m
            swaps += [(a, b), (b, a)]
    z_other = lax.ppermute(z_mine, ("lat", "lon"), swaps)
    pairs = [[2 * m, 2 * m + 1] for m in range(chips)]
    c_both = lax.all_gather(c_mine, "lon", axis_index_groups=pairs)

    moved = pl.pallas_call(
        lambda *refs: main_kernel(blocks, *refs),
        out_shape=jax.ShapeDtypeStruct(circles.shape, jnp.float32),
        in_specs=[vmem] * 9,
        out_specs=vmem,
        scratch_shapes=[
            pltpu.VMEM(circles.shape, jnp.float32),
            pltpu.VMEM((blocks, 2, ROWS, ncol), jnp.float32),
            pltpu.VMEM((2, 10, blocks, ncol), jnp.float32),
            pltpu.VMEM((blocks // 2 + 1, 8 * ROWS, 2 * ncol), jnp.float32),
        ],
        compiler_params=params,
        name="substep",
    )(circles, z_other, c_both, own, tables, limits, twist, forward, inverse)

    home = lax.all_to_all(moved, "lon", split_axis=0, concat_axis=0, tiled=True)
    home = home.reshape(chips, 2, fields, 2, ROWS, ncol).transpose(2, 0, 3, 1, 4, 5)
    return home.reshape(state.shape)


def solution(mesh):
    in_specs = (P(None, None, "lat", "lon"), P(), P())
    out_specs = P(None, None, "lat", "lon")
    return jax.shard_map(
        on_device, mesh=mesh, in_specs=in_specs, out_specs=out_specs, check_vma=False
    )
```

```python
import math

import jax
import jax.numpy as jnp
import numpy as np
from jax import lax
from jax.experimental import pallas as pl
from jax.experimental.pallas import tpu as pltpu
from jax.sharding import PartitionSpec as P

COURANT = 0.05
ROWS = 8
LANES = 128


def row_constants(nlat):
    rows = np.arange(-2, nlat + 2)
    angle = np.float32(math.pi) * ((rows.astype(np.float32) + np.float32(0.5)) / np.float32(nlat) - np.float32(0.5))
    cosine, sine = np.cos(angle.astype(np.float64)), np.sin(angle.astype(np.float64))
    half = 0.5 / cosine[1:-1]
    up, down = cosine[2:] * half, cosine[:-2] * half
    inside = (rows[1:-1] >= 0) & (rows[1:-1] < nlat)
    first, last = np.arange(nlat) % ROWS == 0, np.arange(nlat) % ROWS == ROWS - 1
    own = slice(1, -1)
    polar = (np.arange(nlat) < nlat // 4) | (np.arange(nlat) >= nlat - nlat // 4)
    tiles = [
        half[own],
        np.where(last, 0.0, up[own]),
        np.where(first, 0.0, down[own]),
        2.0 * sine[2:-2],
        cosine[2:-2] ** 2,
        np.where(last, 0.0, 0.5),
        np.where(first, 0.0, 0.5),
        up[own],
        down[own],
        polar.astype(np.float64),
    ]
    tiles = [t.reshape(-1, ROWS) for t in tiles]
    for at in (0, ROWS + 1):
        for v in (half, up, down, np.ones_like(half)):
            edge = (v * inside)[at : at + nlat : ROWS][: nlat // ROWS]
            tiles.append(np.broadcast_to(edge[:, None], (nlat // ROWS, ROWS)))
    table = np.stack(tiles, 1).astype(np.float32)
    return np.ascontiguousarray(np.broadcast_to(table[..., None], table.shape + (LANES,)))


def split(values):
    high = values.astype(jnp.bfloat16)
    low = (values - high.astype(jnp.float32)).astype(jnp.bfloat16)
    return high, low


def fourier_tables(blocks):
    nlon = blocks * LANES
    at = np.arange(LANES)
    phase = 2.0 * np.pi * ((at[:, None] * at[None, :]) % LANES) / LANES
    cos, sin = np.cos(phase), np.sin(phase)
    forward = np.block([[cos, -sin], [sin, cos]])
    inverse = np.block([[cos, sin], [-sin, cos]]) / nlon
    turn = 2.0 * np.pi * np.arange(blocks // 2 + 1)[:, None] * at[None, :] / nlon
    twist = np.stack([np.cos(turn), np.sin(turn)]).astype(np.float32)
    twist = np.broadcast_to(twist[:, :, None, :], (2, blocks // 2 + 1, ROWS, LANES))

    def halves(matrix):
        high = matrix.astype(np.float32).astype(jnp.bfloat16)
        low = (matrix - high.astype(np.float64)).astype(np.float32).astype(jnp.bfloat16)
        return np.stack([high, low])

    return np.ascontiguousarray(twist), halves(forward), halves(inverse)


def root(k, n):
    angle = 2.0 * math.pi * k / n
    return math.cos(angle), math.sin(angle)


def real_fft(x):
    n = len(x)
    if n == 2:
        return [(x[0] + x[1], None), (x[0] - x[1], None)]
    even, odd = real_fft(x[0::2]), real_fft(x[1::2])
    half, quarter = n // 2, n // 4
    out = [None] * (half + 1)
    out[0] = (even[0][0] + odd[0][0], None)
    out[half] = (even[0][0] - odd[0][0], None)
    out[quarter] = (even[quarter][0], -odd[quarter][0])
    for k in range(1, quarter):
        c, s = root(k, n)
        re, im = odd[k]
        t_re, t_im = re * c + im * s, im * c - re * s
        out[k] = (even[k][0] + t_re, even[k][1] + t_im)
        out[half - k] = (even[k][0] - t_re, t_im - even[k][1])
    return out


def real_ifft(w):
    half = len(w) - 1
    n, quarter = 2 * half, half // 2
    if n == 2:
        return [w[0][0] + w[1][0], w[0][0] - w[1][0]]
    even, odd = [None] * (quarter + 1), [None] * (quarter + 1)
    even[0] = (w[0][0] + w[half][0], None)
    odd[0] = (w[0][0] - w[half][0], None)
    even[quarter] = (2.0 * w[quarter][0], None)
    odd[quarter] = (-2.0 * w[quarter][1], None)
    for k in range(1, quarter):
        c, s = root(k, n)
        a, b = w[k], w[half - k]
        even[k] = (a[0] + b[0], a[1] - b[1])
        re, im = a[0] - b[0], a[1] + b[1]
        odd[k] = (re * c - im * s, im * c + re * s)
    x = [None] * n
    x[0::2], x[1::2] = real_ifft(even), real_ifft(odd)
    return x


def spread_kernel(x_ref, out_ref, sems):
    copies = []
    for field in range(4):
        for core in range(2):
            copies.append(
                pltpu.make_async_copy(
                    x_ref.at[field, :, :, core], out_ref.at[:, core, field], sems.at[field, core]
                )
            )
    for copy in copies:
        copy.start()
    for copy in copies:
        copy.wait()


def collect_kernel(x_ref, out_ref, sems):
    copies = []
    for field in range(4):
        for core in range(2):
            copies.append(
                pltpu.make_async_copy(
                    x_ref.at[:, core, field], out_ref.at[field, :, :, core], sems.at[field, core]
                )
            )
    for copy in copies:
        copy.start()
    for copy in copies:
        copy.wait()


def pack_kernel(blocks, x_ref, z_ref, c_ref, own_ref):
    core = lax.axis_index("lon") % 2

    def plane(field, level, row):
        return x_ref[pl.ds((field * 2 + level) * ROWS + row, blocks, stride=8 * ROWS), :]

    for out, end in ((z_ref, core), (c_ref, 1 - core)):
        edge, inner = end * (ROWS - 1), 1 + end * (ROWS - 3)
        for k, (field, row) in enumerate(((0, edge), (1, edge), (3, edge), (2, edge), (2, inner))):
            for level in range(2):
                out[k * 2 + level] = plane(field, level, row)
    for side in range(2):
        for level in range(2):
            own_ref[side * 2 + level] = plane(2, level, side * (ROWS - 1))


def tile(p, g):
    return pl.ds(pl.multiple_of((p * 8 + g) * ROWS, ROWS), ROWS)


def stencil_kernel(blocks, x_ref, tab_ref, damp_ref, inc_ref, div_ref):
    lane = lax.broadcasted_iota(jnp.int32, (ROWS, LANES), 1)
    first_lane, last_lane = lane == 0, lane == LANES - 1

    def zonal_diff(before, here, after):
        east = pltpu.roll(jnp.where(first_lane, after, here), LANES - 1, axis=1)
        west = pltpu.roll(jnp.where(last_lane, before, here), 1, axis=1)
        return (east - west) * tab_ref[0]

    def north(here):
        return pltpu.roll(here, ROWS - 1, axis=0)

    def south(here):
        return pltpu.roll(here, 1, axis=0)

    def merid_flux(here):
        return tab_ref[1] * north(here) - tab_ref[2] * south(here)

    def merid_diff(here):
        return tab_ref[5] * north(here) - tab_ref[6] * south(here)

    def x(p, g):
        return x_ref[tile(p, g), :]

    def around(p):
        return lax.rem(p + blocks - 1, blocks), lax.rem(p + 1, blocks)

    def divergence(p, carry):
        before, after = around(p)
        for level in range(2):
            u, v = 2 + level, 4 + level
            div_ref[p, level] = zonal_diff(x(before, u), x(p, u), x(after, u)) + merid_flux(x(p, v))
        return carry

    lax.fori_loop(0, blocks, divergence, 0, unroll=4)

    def increments(p, carry):
        before, after = around(p)
        for level in range(2):
            h, u, v, t = level, 2 + level, 4 + level, 6 + level
            damp = tab_ref[4] * damp_ref[level]
            thick, zonal, merid, potential = x(p, h), x(p, u), x(p, v), x(p, t)
            thick_b, thick_a = x(before, h), x(after, h)
            carried = 1.0 + thick
            flux_b, flux_a = (1.0 + thick_b) * x(before, u), (1.0 + thick_a) * x(after, u)
            inc_ref[tile(p, h), :] = -COURANT * (
                zonal_diff(flux_b, carried * zonal, flux_a) + merid_flux(carried * merid)
            )
            div = div_ref[p, level]
            inc_ref[tile(p, u), :] = COURANT * (
                tab_ref[3] * merid - zonal_diff(thick_b, thick, thick_a)
            ) + damp * zonal_diff(div_ref[before, level], div, div_ref[after, level])
            inc_ref[tile(p, v), :] = damp * merid_diff(div) - COURANT * (
                tab_ref[3] * zonal + merid_diff(thick)
            )
            inc_ref[tile(p, t), :] = -COURANT * (
                zonal * zonal_diff(x(before, t), potential, x(after, t))
                + merid * merid_diff(potential)
            )
        return carry

    lax.fori_loop(0, blocks, increments, 0, unroll=2)


def filter_kernel(
    blocks,
    x_ref,
    inc_ref,
    z_ref,
    c_ref,
    own_ref,
    tab_ref,
    damp_ref,
    limit_ref,
    twist_ref,
    forward_ref,
    inverse_ref,
    out_ref,
    wave_ref,
):
    del inc_ref
    core = lax.axis_index("lon") % 2
    lane = lax.broadcasted_iota(jnp.int32, (blocks, LANES), 1)

    def shifted_diff(v):
        after = jnp.where(lane == 0, pltpu.roll(v, blocks - 1, axis=0), v)
        before = jnp.where(lane == LANES - 1, pltpu.roll(v, 1, axis=0), v)
        return pltpu.roll(after, LANES - 1, axis=1) - pltpu.roll(before, 1, axis=1)

    def add(group, row, value):
        rows = pl.ds(group * ROWS + row, blocks, stride=8 * ROWS)
        out_ref[rows, :] = out_ref[rows, :] + value

    for side in range(2):
        edge, inner = side * (ROWS - 1), 1 + side * (ROWS - 3)
        half, up, down, inside = (tab_ref[10 + side * 4 + i, :1] for i in range(4))
        weight = tab_ref[8 - side, edge : edge + 1] * (1.0 if side else -1.0)
        step = 0.5 if side else -0.5
        for level in range(2):
            damp = tab_ref[4] * damp_ref[level]
            damp_edge, damp_inner = damp[edge : edge + 1], damp[inner : inner + 1]

            def beyond(k):
                other = c_ref[1 - core, k * 2 + level]
                return jnp.where(core == side, z_ref[k * 2 + level], other) * inside

            thick, zonal, potential, near, far = (beyond(k) for k in range(5))
            own = own_ref[side * 2 + level]
            above, below = (far, own) if side else (own, far)
            div = shifted_diff(zonal) * half + up * above - down * below
            more = weight * near
            add(level, edge, -COURANT * weight * ((1.0 + thick) * near))
            add(2 + level, edge, damp_edge * tab_ref[0, edge : edge + 1] * shifted_diff(more))
            add(4 + level, edge, step * (damp_edge * div - COURANT * thick))
            add(4 + level, inner, step * damp_inner * more)
            add(6 + level, edge, -COURANT * step * (own * potential))

    polar = tab_ref[9]
    top = blocks // 2
    nlon = blocks * LANES

    @pl.when(jnp.max(polar) == 0)
    def _():
        out_ref[...] = x_ref[...] + out_ref[...]

    @pl.when(jnp.max(polar) > 0)
    def _():
        def analyse(g, carry):
            waves = real_fft([out_ref[tile(p, g), :] for p in range(blocks)])
            rows = pl.ds(pl.multiple_of(g * ROWS, ROWS), ROWS)
            for k, (re, im) in enumerate(waves):
                c, s = twist_ref[0, k], twist_ref[1, k]
                if im is None:
                    turned = (re, jnp.zeros_like(re)) if k == 0 else (re * c, -(re * s))
                else:
                    turned = (re * c + im * s, im * c - re * s)
                wave_ref[k, rows, :LANES], wave_ref[k, rows, LANES:] = turned
            return carry

        lax.fori_loop(0, 8, analyse, 0)

        def product(values, table_ref):
            high, low = split(values)
            dot = lambda a, b: jnp.dot(a, b, preferred_element_type=jnp.float32)
            return dot(high, table_ref[0]) + dot(low, table_ref[0]) + dot(high, table_ref[1])

        count = (top + 1) * 8 * ROWS
        spectrum = product(wave_ref[...].reshape(count, 2 * LANES), forward_ref)
        spectrum = spectrum.reshape(top + 1, 8, ROWS, 2 * LANES)
        wave = lax.broadcasted_iota(jnp.int32, (top + 1, 1, ROWS, LANES), 0)
        wave = wave + blocks * lax.broadcasted_iota(jnp.int32, (top + 1, 1, ROWS, LANES), 3)
        kept = jnp.minimum(wave, nlon - wave) <= limit_ref[...]
        kept = jnp.concatenate([kept, kept], axis=-1)
        spectrum = jnp.where(kept, spectrum, 0.0).reshape(count, 2 * LANES)
        wave_ref[...] = product(spectrum, inverse_ref).reshape(top + 1, 8 * ROWS, 2 * LANES)

        def rebuild(g, carry):
            rows = pl.ds(pl.multiple_of(g * ROWS, ROWS), ROWS)
            waves = []
            for k in range(top + 1):
                re, im = wave_ref[k, rows, :LANES], wave_ref[k, rows, LANES:]
                c, s = twist_ref[0, k], twist_ref[1, k]
                if k == 0:
                    waves.append((re, None))
                elif k == top:
                    waves.append((re * c - im * s, None))
                else:
                    waves.append((re * c - im * s, im * c + re * s))
            for p, smooth in enumerate(real_ifft(waves)):
                at = tile(p, g)
                out_ref[at, :] = x_ref[at, :] + jnp.where(polar > 0, smooth, out_ref[at, :])
            return carry

        lax.fori_loop(0, 8, rebuild, 0)


def on_device(state, damping, cutoff):
    fields, levels, nrow, ncol = state.shape
    bands, blocks = lax.axis_size("lat"), lax.axis_size("lon")
    lat, lon = lax.axis_index("lat"), lax.axis_index("lon")
    chips = blocks // 2
    vmem, hbm = pl.BlockSpec(memory_space=pltpu.VMEM), pl.BlockSpec(memory_space=pltpu.HBM)
    params = pltpu.CompilerParams(vmem_limit_bytes=40 * 2**20)

    def call(kernel, name, out, ins, outs, cost, scratch=(), aliases=None):
        return pl.pallas_call(
            kernel,
            out_shape=out,
            in_specs=ins,
            out_specs=outs,
            scratch_shapes=scratch,
            compiler_params=params,
            input_output_aliases=aliases or {},
            cost_estimate=pl.CostEstimate(flops=cost, bytes_accessed=2**22, transcendentals=0),
            name=name,
        )

    def array(*shape):
        return jax.ShapeDtypeStruct(shape, jnp.float32)

    sems = [pltpu.SemaphoreType.DMA((fields, 2))]
    parts = call(
        spread_kernel, "spread", array(chips, 2, fields, 2, ROWS, ncol), [hbm], vmem, 0, sems
    )(state.reshape(fields, chips, 2, 2, ROWS, ncol))
    circles = lax.all_to_all(
        parts.reshape(blocks, -1, ncol), "lon", split_axis=0, concat_axis=0, tiled=True
    ).reshape(-1, ncol)

    group = lat * (nrow // ROWS) + lon % 2
    tables = lax.dynamic_index_in_dim(row_constants(nrow * bands), group, keepdims=False)
    damp = lax.dynamic_slice(damping, (lon // 2 * 2,), (2,))
    damp = jnp.broadcast_to(damp[:, None, None], (2, ROWS, ncol))
    limit = lax.dynamic_slice(cutoff, (group * ROWS,), (ROWS,))
    limit = jnp.broadcast_to(limit[:, None], (ROWS, ncol))
    twist, forward, inverse = fourier_tables(blocks)

    plane = array(10, blocks, ncol)
    z_mine, c_mine, own = call(
        lambda *refs: pack_kernel(blocks, *refs),
        "pack",
        (plane, plane, array(4, blocks, ncol)),
        [vmem],
        (vmem, vmem, vmem),
        0,
    )(circles)

    swaps = []
    for z in range(bands - 1):
        for m in range(chips):
            a, b = z * blocks + 2 * m + 1, (z + 1) * blocks + 2 * m
            swaps += [(a, b), (b, a)]
    z_other = lax.ppermute(z_mine, ("lat", "lon"), swaps)
    pairs = [[2 * m, 2 * m + 1] for m in range(chips)]
    c_both = lax.all_gather(c_mine, "lon", axis_index_groups=pairs)
    increments = call(
        lambda *refs: stencil_kernel(blocks, *refs),
        "stencil",
        array(*circles.shape),
        [vmem] * 3,
        vmem,
        2**31,
        [pltpu.VMEM((blocks, 2, ROWS, ncol), jnp.float32)],
    )(circles, tables, damp)
    moved = call(
        lambda *refs: filter_kernel(blocks, *refs),
        "filter",
        array(*circles.shape),
        [vmem] * 11,
        vmem,
        2**31,
        [pltpu.VMEM((blocks // 2 + 1, 8 * ROWS, 2 * ncol), jnp.float32)],
        {1: 0},
    )(circles, increments, z_other, c_both, own, tables, damp, limit, twist, forward, inverse)

    home = lax.all_to_all(
        moved.reshape(blocks, -1, ncol), "lon", split_axis=0, concat_axis=0, tiled=True
    )
    out = call(
        collect_kernel, "collect", array(fields, chips, 2, 2, ROWS, ncol), [vmem], hbm, 0, sems
    )(home.reshape(chips, 2, fields, 2, ROWS, ncol))
    return out.reshape(state.shape)


def solution(mesh):
    in_specs = (P(None, None, "lat", "lon"), P(), P())
    out_specs = P(None, None, "lat", "lon")
    return jax.shard_map(
        on_device, mesh=mesh, in_specs=in_specs, out_specs=out_specs, check_vma=False
    )
```

```python
import math

import jax
import jax.numpy as jnp
import numpy as np
from jax import lax
from jax.experimental import pallas as pl
from jax.experimental.pallas import tpu as pltpu
from jax.sharding import PartitionSpec as P

COURANT = 0.05
ROWS = 8
LANES = 128


def sine(angle):
    square = angle * angle
    total = jnp.zeros_like(angle)
    for n in (13, 11, 9, 7, 5, 3, 1):
        total = total * square + (-1.0) ** (n // 2) / math.factorial(n)
    return total * angle


class Rows:
    def __init__(self, bands):
        self.core = lax.axis_index("lon") % 2
        self.first = (lax.axis_index("lat") * 2 + self.core) * ROWS
        self.nlat = nlat = bands * 2 * ROWS
        row = lax.broadcasted_iota(jnp.int32, (ROWS, LANES), 0)
        near = self.first + row
        at = self.cosine(near)
        self.half = 0.5 / at
        self.up, self.down = self.cosine(near + 1) * self.half, self.cosine(near - 1) * self.half
        middle = near.astype(jnp.float32) + (0.5 - 0.5 * nlat)
        self.coriolis = 2.0 * sine(middle * (math.pi / nlat))
        self.square = at * at
        self.polar = (near < nlat // 4) | (near >= nlat - nlat // 4)
        ends = self.first + jnp.where(row < 3, row - 2, row + ROWS - 4)
        self.ends = self.cosine(ends)

    def cosine(self, row):
        index = row.astype(jnp.float32) + 0.5
        return sine(jnp.minimum(index, self.nlat - index) * (math.pi / self.nlat))

    def beside(self, side):
        below, at, above = (self.ends[side * 3 + i : side * 3 + i + 1] for i in range(3))
        row = self.first + (ROWS if side else -1)
        inside = ((row >= 0) & (row < self.nlat)).astype(jnp.float32)
        half = 0.5 / at * inside
        return half, above * half, below * half, inside


def split(values):
    high = values.astype(jnp.bfloat16)
    low = (values - high.astype(jnp.float32)).astype(jnp.bfloat16)
    return high, low


def fourier_tables(blocks):
    nlon = blocks * LANES
    at = np.arange(LANES)
    phase = 2.0 * np.pi * ((at[:, None] * at[None, :]) % LANES) / LANES
    cos, sin = np.cos(phase), np.sin(phase)
    forward = np.block([[cos, -sin], [sin, cos]])
    inverse = np.block([[cos, sin], [-sin, cos]]) / nlon
    turn = 2.0 * np.pi * np.arange(blocks // 2 + 1)[:, None] * at[None, :] / nlon
    twist = np.stack([np.cos(turn), np.sin(turn)]).astype(np.float32)
    twist = np.broadcast_to(twist[:, :, None, :], (2, blocks // 2 + 1, ROWS, LANES))

    def halves(matrix):
        high = matrix.astype(np.float32).astype(jnp.bfloat16)
        low = (matrix - high.astype(np.float64)).astype(np.float32).astype(jnp.bfloat16)
        return np.stack([high, low])

    return np.ascontiguousarray(twist), halves(forward), halves(inverse)


def root(k, n):
    angle = 2.0 * math.pi * k / n
    return math.cos(angle), math.sin(angle)


def real_fft(x):
    n = len(x)
    if n == 2:
        return [(x[0] + x[1], None), (x[0] - x[1], None)]
    even, odd = real_fft(x[0::2]), real_fft(x[1::2])
    half, quarter = n // 2, n // 4
    out = [None] * (half + 1)
    out[0] = (even[0][0] + odd[0][0], None)
    out[half] = (even[0][0] - odd[0][0], None)
    out[quarter] = (even[quarter][0], -odd[quarter][0])
    for k in range(1, quarter):
        c, s = root(k, n)
        re, im = odd[k]
        t_re, t_im = re * c + im * s, im * c - re * s
        out[k] = (even[k][0] + t_re, even[k][1] + t_im)
        out[half - k] = (even[k][0] - t_re, t_im - even[k][1])
    return out


def real_ifft(w):
    half = len(w) - 1
    n, quarter = 2 * half, half // 2
    if n == 2:
        return [w[0][0] + w[1][0], w[0][0] - w[1][0]]
    even, odd = [None] * (quarter + 1), [None] * (quarter + 1)
    even[0] = (w[0][0] + w[half][0], None)
    odd[0] = (w[0][0] - w[half][0], None)
    even[quarter] = (2.0 * w[quarter][0], None)
    odd[quarter] = (-2.0 * w[quarter][1], None)
    for k in range(1, quarter):
        c, s = root(k, n)
        a, b = w[k], w[half - k]
        even[k] = (a[0] + b[0], a[1] - b[1])
        re, im = a[0] - b[0], a[1] + b[1]
        odd[k] = (re * c - im * s, im * c + re * s)
    x = [None] * n
    x[0::2], x[1::2] = real_ifft(even), real_ifft(odd)
    return x


def spread_kernel(x_ref, out_ref, sems):
    copies = []
    for field in range(4):
        for core in range(2):
            copies.append(
                pltpu.make_async_copy(
                    x_ref.at[field, :, :, core], out_ref.at[:, core, field], sems.at[field, core]
                )
            )
    for copy in copies:
        copy.start()
    for copy in copies:
        copy.wait()


def collect_kernel(x_ref, out_ref, sems):
    copies = []
    for field in range(4):
        for core in range(2):
            copies.append(
                pltpu.make_async_copy(
                    x_ref.at[:, core, field], out_ref.at[field, :, :, core], sems.at[field, core]
                )
            )
    for copy in copies:
        copy.start()
    for copy in copies:
        copy.wait()


def pack_kernel(blocks, x_ref, z_ref, c_ref, own_ref):
    core = lax.axis_index("lon") % 2

    def plane(field, level, row):
        return x_ref[pl.ds((field * 2 + level) * ROWS + row, blocks, stride=8 * ROWS), :]

    for out, end in ((z_ref, core), (c_ref, 1 - core)):
        edge, inner = end * (ROWS - 1), 1 + end * (ROWS - 3)
        for k, (field, row) in enumerate(((0, edge), (1, edge), (3, edge), (2, edge), (2, inner))):
            for level in range(2):
                out[k * 2 + level] = plane(field, level, row)
    for side in range(2):
        for level in range(2):
            own_ref[side * 2 + level] = plane(2, level, side * (ROWS - 1))


def parameters(rows, damp_ref, cutoff_ref, param_ref):
    level = lax.axis_index("lon") // 2 * 2
    damping = damp_ref[...].reshape(1, -1)
    at = lax.broadcasted_iota(jnp.int32, damping.shape, 1)
    for i in range(2):
        one = jnp.sum(jnp.where(at == level + i, damping, 0.0), axis=1, keepdims=True)
        param_ref[i] = jnp.broadcast_to(one, (ROWS, LANES))
    cutoff = cutoff_ref[...].astype(jnp.float32).reshape(1, -1)
    cutoff = jnp.broadcast_to(cutoff, (ROWS, cutoff.shape[1]))
    at = lax.broadcasted_iota(jnp.int32, cutoff.shape, 1)
    row = lax.broadcasted_iota(jnp.int32, cutoff.shape, 0)
    limit = jnp.sum(jnp.where(at == rows.first + row, cutoff, 0.0), axis=1, keepdims=True)
    param_ref[2] = jnp.broadcast_to(limit, (ROWS, LANES))


def tile(p, g):
    return pl.ds(pl.multiple_of((p * 8 + g) * ROWS, ROWS), ROWS)


def stencil_kernel(bands, blocks, x_ref, damp_ref, cutoff_ref, inc_ref, param_ref, div_ref):
    rows = Rows(bands)
    parameters(rows, damp_ref, cutoff_ref, param_ref)
    row = lax.broadcasted_iota(jnp.int32, (ROWS, LANES), 0)
    up = jnp.where(row == ROWS - 1, 0.0, rows.up)
    down = jnp.where(row == 0, 0.0, rows.down)
    half_up = jnp.where(row == ROWS - 1, 0.0, 0.5)
    half_down = jnp.where(row == 0, 0.0, 0.5)
    damping = [rows.square * param_ref[i] for i in range(2)]
    lane = lax.broadcasted_iota(jnp.int32, (ROWS, LANES), 1)
    first_lane, last_lane = lane == 0, lane == LANES - 1

    def zonal_diff(before, here, after):
        east = pltpu.roll(jnp.where(first_lane, after, here), LANES - 1, axis=1)
        west = pltpu.roll(jnp.where(last_lane, before, here), 1, axis=1)
        return (east - west) * rows.half

    def north(here):
        return pltpu.roll(here, ROWS - 1, axis=0)

    def south(here):
        return pltpu.roll(here, 1, axis=0)

    def merid_flux(here):
        return up * north(here) - down * south(here)

    def merid_diff(here):
        return half_up * north(here) - half_down * south(here)

    def x(p, g):
        return x_ref[tile(p, g), :]

    def around(p):
        return lax.rem(p + blocks - 1, blocks), lax.rem(p + 1, blocks)

    def divergence(p, carry):
        before, after = around(p)
        for level in range(2):
            u, v = 2 + level, 4 + level
            div_ref[p, level] = zonal_diff(x(before, u), x(p, u), x(after, u)) + merid_flux(x(p, v))
        return carry

    lax.fori_loop(0, blocks, divergence, 0, unroll=4)

    def increments(p, carry):
        before, after = around(p)
        for level in range(2):
            h, u, v, t = level, 2 + level, 4 + level, 6 + level
            damp = damping[level]
            thick, zonal, merid, potential = x(p, h), x(p, u), x(p, v), x(p, t)
            thick_b, thick_a = x(before, h), x(after, h)
            carried = 1.0 + thick
            flux_b, flux_a = (1.0 + thick_b) * x(before, u), (1.0 + thick_a) * x(after, u)
            inc_ref[tile(p, h), :] = -COURANT * (
                zonal_diff(flux_b, carried * zonal, flux_a) + merid_flux(carried * merid)
            )
            div = div_ref[p, level]
            inc_ref[tile(p, u), :] = COURANT * (
                rows.coriolis * merid - zonal_diff(thick_b, thick, thick_a)
            ) + damp * zonal_diff(div_ref[before, level], div, div_ref[after, level])
            inc_ref[tile(p, v), :] = damp * merid_diff(div) - COURANT * (
                rows.coriolis * zonal + merid_diff(thick)
            )
            inc_ref[tile(p, t), :] = -COURANT * (
                zonal * zonal_diff(x(before, t), potential, x(after, t))
                + merid * merid_diff(potential)
            )
        return carry

    lax.fori_loop(0, blocks, increments, 0, unroll=2)


def filter_kernel(
    bands,
    blocks,
    x_ref,
    inc_ref,
    z_ref,
    c_ref,
    own_ref,
    param_ref,
    twist_ref,
    forward_ref,
    inverse_ref,
    out_ref,
    wave_ref,
):
    del inc_ref
    rows = Rows(bands)
    damping = [rows.square * param_ref[i] for i in range(2)]
    lane = lax.broadcasted_iota(jnp.int32, (blocks, LANES), 1)

    def shifted_diff(v):
        after = jnp.where(lane == 0, pltpu.roll(v, blocks - 1, axis=0), v)
        before = jnp.where(lane == LANES - 1, pltpu.roll(v, 1, axis=0), v)
        return pltpu.roll(after, LANES - 1, axis=1) - pltpu.roll(before, 1, axis=1)

    def add(group, row, value):
        at = pl.ds(group * ROWS + row, blocks, stride=8 * ROWS)
        out_ref[at, :] = out_ref[at, :] + value

    for side in range(2):
        edge, inner = side * (ROWS - 1), 1 + side * (ROWS - 3)
        half, up, down, inside = rows.beside(side)
        weight = rows.up[edge : edge + 1] if side else -rows.down[edge : edge + 1]
        step = 0.5 if side else -0.5
        for level in range(2):
            damp = damping[level]
            damp_edge, damp_inner = damp[edge : edge + 1], damp[inner : inner + 1]

            def beyond(k):
                other = c_ref[1 - rows.core, k * 2 + level]
                return jnp.where(rows.core == side, z_ref[k * 2 + level], other) * inside

            thick, zonal, potential, near, far = (beyond(k) for k in range(5))
            own = own_ref[side * 2 + level]
            above, below = (far, own) if side else (own, far)
            div = shifted_diff(zonal) * half + up * above - down * below
            more = weight * near
            add(level, edge, -COURANT * weight * ((1.0 + thick) * near))
            add(2 + level, edge, damp_edge * rows.half[edge : edge + 1] * shifted_diff(more))
            add(4 + level, edge, step * (damp_edge * div - COURANT * thick))
            add(4 + level, inner, step * damp_inner * more)
            add(6 + level, edge, -COURANT * step * (own * potential))

    polar = rows.polar
    limit = param_ref[2].astype(jnp.int32)
    any_polar = (rows.first < rows.nlat // 4) | (rows.first + ROWS > rows.nlat - rows.nlat // 4)
    top = blocks // 2
    nlon = blocks * LANES

    @pl.when(jnp.logical_not(any_polar))
    def _():
        out_ref[...] = x_ref[...] + out_ref[...]

    @pl.when(any_polar)
    def _():
        def analyse(g, carry):
            waves = real_fft([out_ref[tile(p, g), :] for p in range(blocks)])
            at = pl.ds(pl.multiple_of(g * ROWS, ROWS), ROWS)
            for k, (re, im) in enumerate(waves):
                c, s = twist_ref[0, k], twist_ref[1, k]
                if im is None:
                    turned = (re, jnp.zeros_like(re)) if k == 0 else (re * c, -(re * s))
                else:
                    turned = (re * c + im * s, im * c - re * s)
                wave_ref[k, at, :LANES], wave_ref[k, at, LANES:] = turned
            return carry

        lax.fori_loop(0, 8, analyse, 0)

        def product(values, table_ref):
            high, low = split(values)
            dot = lambda a, b: jnp.dot(a, b, preferred_element_type=jnp.float32)
            return dot(high, table_ref[0]) + dot(low, table_ref[0]) + dot(high, table_ref[1])

        count = (top + 1) * 8 * ROWS
        spectrum = product(wave_ref[...].reshape(count, 2 * LANES), forward_ref)
        spectrum = spectrum.reshape(top + 1, 8, ROWS, 2 * LANES)
        wave = lax.broadcasted_iota(jnp.int32, (top + 1, 1, ROWS, LANES), 0)
        wave = wave + blocks * lax.broadcasted_iota(jnp.int32, (top + 1, 1, ROWS, LANES), 3)
        kept = jnp.minimum(wave, nlon - wave) <= limit
        kept = jnp.concatenate([kept, kept], axis=-1)
        spectrum = jnp.where(kept, spectrum, 0.0).reshape(count, 2 * LANES)
        wave_ref[...] = product(spectrum, inverse_ref).reshape(top + 1, 8 * ROWS, 2 * LANES)

        def rebuild(g, carry):
            at = pl.ds(pl.multiple_of(g * ROWS, ROWS), ROWS)
            waves = []
            for k in range(top + 1):
                re, im = wave_ref[k, at, :LANES], wave_ref[k, at, LANES:]
                c, s = twist_ref[0, k], twist_ref[1, k]
                if k == 0:
                    waves.append((re, None))
                elif k == top:
                    waves.append((re * c - im * s, None))
                else:
                    waves.append((re * c - im * s, im * c + re * s))
            for p, smooth in enumerate(real_ifft(waves)):
                here = tile(p, g)
                out_ref[here, :] = x_ref[here, :] + jnp.where(polar, smooth, out_ref[here, :])
            return carry

        lax.fori_loop(0, 8, rebuild, 0)


def on_device(state, damping, cutoff):
    fields, levels, nrow, ncol = state.shape
    bands, blocks = lax.axis_size("lat"), lax.axis_size("lon")
    chips = blocks // 2
    vmem, hbm = pl.BlockSpec(memory_space=pltpu.VMEM), pl.BlockSpec(memory_space=pltpu.HBM)
    limits = pltpu.CompilerParams(vmem_limit_bytes=40 * 2**20)

    def call(kernel, name, out, ins, outs, cost, scratch=(), aliases=None):
        return pl.pallas_call(
            kernel,
            out_shape=out,
            in_specs=ins,
            out_specs=outs,
            scratch_shapes=scratch,
            compiler_params=limits,
            input_output_aliases=aliases or {},
            cost_estimate=pl.CostEstimate(flops=cost, bytes_accessed=2**22, transcendentals=0),
            name=name,
        )

    def array(*shape):
        return jax.ShapeDtypeStruct(shape, jnp.float32)

    sems = [pltpu.SemaphoreType.DMA((fields, 2))]
    parts = call(
        spread_kernel, "spread", array(chips, 2, fields, 2, ROWS, ncol), [hbm], vmem, 0, sems
    )(state.reshape(fields, chips, 2, 2, ROWS, ncol))
    circles = lax.all_to_all(
        parts.reshape(blocks, -1, ncol), "lon", split_axis=0, concat_axis=0, tiled=True
    ).reshape(-1, ncol)

    twist, forward, inverse = fourier_tables(blocks)

    plane = array(10, blocks, ncol)
    z_mine, c_mine, own = call(
        lambda *refs: pack_kernel(blocks, *refs),
        "pack",
        (plane, plane, array(4, blocks, ncol)),
        [vmem],
        (vmem, vmem, vmem),
        0,
    )(circles)

    swaps = []
    for z in range(bands - 1):
        for m in range(chips):
            a, b = z * blocks + 2 * m + 1, (z + 1) * blocks + 2 * m
            swaps += [(a, b), (b, a)]
    z_other = lax.ppermute(z_mine, ("lat", "lon"), swaps)
    pairs = [[2 * m, 2 * m + 1] for m in range(chips)]
    c_both = lax.all_gather(c_mine, "lon", axis_index_groups=pairs)
    increments, params = call(
        lambda *refs: stencil_kernel(bands, blocks, *refs),
        "stencil",
        (array(*circles.shape), array(3, ROWS, ncol)),
        [vmem] * 3,
        (vmem, vmem),
        2**31,
        [pltpu.VMEM((blocks, 2, ROWS, ncol), jnp.float32)],
    )(circles, damping, cutoff)
    moved = call(
        lambda *refs: filter_kernel(bands, blocks, *refs),
        "filter",
        array(*circles.shape),
        [vmem] * 9,
        vmem,
        2**31,
        [pltpu.VMEM((blocks // 2 + 1, 8 * ROWS, 2 * ncol), jnp.float32)],
        {1: 0},
    )(circles, increments, z_other, c_both, own, params, twist, forward, inverse)

    home = lax.all_to_all(
        moved.reshape(blocks, -1, ncol), "lon", split_axis=0, concat_axis=0, tiled=True
    )
    out = call(
        collect_kernel, "collect", array(fields, chips, 2, 2, ROWS, ncol), [vmem], hbm, 0, sems
    )(home.reshape(chips, 2, fields, 2, ROWS, ncol))
    return out.reshape(state.shape)


def solution(mesh):
    in_specs = (P(None, None, "lat", "lon"), P(), P())
    out_specs = P(None, None, "lat", "lon")
    return jax.shard_map(
        on_device, mesh=mesh, in_specs=in_specs, out_specs=out_specs, check_vma=False
    )
```

```python
import math

import jax
import jax.numpy as jnp
import numpy as np
from jax import lax
from jax.experimental import pallas as pl
from jax.experimental.pallas import tpu as pltpu
from jax.sharding import PartitionSpec as P

COURANT = 0.05
ROWS = 8
LANES = 128


def sine(angle):
    square = angle * angle
    total = jnp.zeros_like(angle)
    for n in (13, 11, 9, 7, 5, 3, 1):
        total = total * square + (-1.0) ** (n // 2) / math.factorial(n)
    return total * angle


class Rows:
    def __init__(self, bands):
        self.core = lax.axis_index("lon") % 2
        self.first = (lax.axis_index("lat") * 2 + self.core) * ROWS
        self.nlat = nlat = bands * 2 * ROWS
        row = lax.broadcasted_iota(jnp.int32, (ROWS, LANES), 0)
        near = self.first + row
        at = self.cosine(near)
        self.half = 0.5 / at
        self.up, self.down = self.cosine(near + 1) * self.half, self.cosine(near - 1) * self.half
        middle = near.astype(jnp.float32) + (0.5 - 0.5 * nlat)
        self.coriolis = 2.0 * sine(middle * (math.pi / nlat))
        self.square = at * at
        self.polar = (near < nlat // 4) | (near >= nlat - nlat // 4)
        ends = self.first + jnp.where(row < 3, row - 2, row + ROWS - 4)
        self.ends = self.cosine(ends)

    def cosine(self, row):
        index = row.astype(jnp.float32) + 0.5
        return sine(jnp.minimum(index, self.nlat - index) * (math.pi / self.nlat))

    def beside(self, side):
        below, at, above = (self.ends[side * 3 + i : side * 3 + i + 1] for i in range(3))
        row = self.first + (ROWS if side else -1)
        inside = ((row >= 0) & (row < self.nlat)).astype(jnp.float32)
        half = 0.5 / at * inside
        return half, above * half, below * half, inside


def split(values):
    high = values.astype(jnp.bfloat16)
    low = (values - high.astype(jnp.float32)).astype(jnp.bfloat16)
    return high, low


def fourier_tables(blocks):
    nlon = blocks * LANES
    at = np.arange(LANES)
    phase = 2.0 * np.pi * ((at[:, None] * at[None, :]) % LANES) / LANES
    cos, sin = np.cos(phase), np.sin(phase)
    forward = np.block([[cos, -sin], [sin, cos]])
    inverse = np.block([[cos, sin], [-sin, cos]]) / nlon
    turn = 2.0 * np.pi * np.arange(blocks // 2 + 1)[:, None] * at[None, :] / nlon
    twist = np.stack([np.cos(turn), np.sin(turn)]).astype(np.float32)
    twist = np.broadcast_to(twist[:, :, None, :], (2, blocks // 2 + 1, ROWS, LANES))

    def halves(matrix):
        high = matrix.astype(np.float32).astype(jnp.bfloat16)
        low = (matrix - high.astype(np.float64)).astype(np.float32).astype(jnp.bfloat16)
        return np.stack([high, low])

    return np.ascontiguousarray(twist), halves(forward), halves(inverse)


def root(k, n):
    angle = 2.0 * math.pi * k / n
    return math.cos(angle), math.sin(angle)


def real_fft(x):
    n = len(x)
    if n == 2:
        return [(x[0] + x[1], None), (x[0] - x[1], None)]
    even, odd = real_fft(x[0::2]), real_fft(x[1::2])
    half, quarter = n // 2, n // 4
    out = [None] * (half + 1)
    out[0] = (even[0][0] + odd[0][0], None)
    out[half] = (even[0][0] - odd[0][0], None)
    out[quarter] = (even[quarter][0], -odd[quarter][0])
    for k in range(1, quarter):
        c, s = root(k, n)
        re, im = odd[k]
        t_re, t_im = re * c + im * s, im * c - re * s
        out[k] = (even[k][0] + t_re, even[k][1] + t_im)
        out[half - k] = (even[k][0] - t_re, t_im - even[k][1])
    return out


def real_ifft(w):
    half = len(w) - 1
    n, quarter = 2 * half, half // 2
    if n == 2:
        return [w[0][0] + w[1][0], w[0][0] - w[1][0]]
    even, odd = [None] * (quarter + 1), [None] * (quarter + 1)
    even[0] = (w[0][0] + w[half][0], None)
    odd[0] = (w[0][0] - w[half][0], None)
    even[quarter] = (2.0 * w[quarter][0], None)
    odd[quarter] = (-2.0 * w[quarter][1], None)
    for k in range(1, quarter):
        c, s = root(k, n)
        a, b = w[k], w[half - k]
        even[k] = (a[0] + b[0], a[1] - b[1])
        re, im = a[0] - b[0], a[1] + b[1]
        odd[k] = (re * c - im * s, im * c + re * s)
    x = [None] * n
    x[0::2], x[1::2] = real_ifft(even), real_ifft(odd)
    return x


def spread_kernel(x_ref, out_ref, sems):
    copies = []
    for field in range(4):
        for core in range(2):
            copies.append(
                pltpu.make_async_copy(
                    x_ref.at[field, :, :, core], out_ref.at[:, core, field], sems.at[field, core]
                )
            )
    for copy in copies:
        copy.start()
    for copy in copies:
        copy.wait()


def collect_kernel(x_ref, out_ref, sems):
    copies = []
    for field in range(4):
        for core in range(2):
            copies.append(
                pltpu.make_async_copy(
                    x_ref.at[:, core, field], out_ref.at[field, :, :, core], sems.at[field, core]
                )
            )
    for copy in copies:
        copy.start()
    for copy in copies:
        copy.wait()


def pack_kernel(blocks, x_ref, z_ref, c_ref, own_ref):
    core = lax.axis_index("lon") % 2

    def plane(field, level, row):
        return x_ref[pl.ds((field * 2 + level) * ROWS + row, blocks, stride=8 * ROWS), :]

    for out, end in ((z_ref, core), (c_ref, 1 - core)):
        edge, inner = end * (ROWS - 1), 1 + end * (ROWS - 3)
        for k, (field, row) in enumerate(((0, edge), (1, edge), (3, edge), (2, edge), (2, inner))):
            for level in range(2):
                out[k * 2 + level] = plane(field, level, row)
    for side in range(2):
        for level in range(2):
            own_ref[side * 2 + level] = plane(2, level, side * (ROWS - 1))


def parameters(rows, damp_ref, cutoff_ref, param_ref):
    level = lax.axis_index("lon") // 2 * 2
    damping = damp_ref[...].reshape(1, -1)
    at = lax.broadcasted_iota(jnp.int32, damping.shape, 1)
    for i in range(2):
        one = jnp.sum(jnp.where(at == level + i, damping, 0.0), axis=1, keepdims=True)
        param_ref[i] = jnp.broadcast_to(one, (ROWS, LANES))
    cutoff = cutoff_ref[...].astype(jnp.float32).reshape(1, -1)
    cutoff = jnp.broadcast_to(cutoff, (ROWS, cutoff.shape[1]))
    at = lax.broadcasted_iota(jnp.int32, cutoff.shape, 1)
    row = lax.broadcasted_iota(jnp.int32, cutoff.shape, 0)
    limit = jnp.sum(jnp.where(at == rows.first + row, cutoff, 0.0), axis=1, keepdims=True)
    param_ref[2] = jnp.broadcast_to(limit, (ROWS, LANES))


def tile(p, g):
    return pl.ds(pl.multiple_of((p * 8 + g) * ROWS, ROWS), ROWS)


def stencil_kernel(bands, blocks, x_ref, damp_ref, cutoff_ref, inc_ref, param_ref, div_ref):
    rows = Rows(bands)
    parameters(rows, damp_ref, cutoff_ref, param_ref)
    row = lax.broadcasted_iota(jnp.int32, (ROWS, LANES), 0)
    up = jnp.where(row == ROWS - 1, 0.0, rows.up)
    down = jnp.where(row == 0, 0.0, rows.down)
    half_up = jnp.where(row == ROWS - 1, 0.0, 0.5)
    half_down = jnp.where(row == 0, 0.0, 0.5)
    damping = [rows.square * param_ref[i] for i in range(2)]
    lane = lax.broadcasted_iota(jnp.int32, (ROWS, LANES), 1)
    first_lane, last_lane = lane == 0, lane == LANES - 1

    def zonal_diff(before, here, after):
        east = pltpu.roll(jnp.where(first_lane, after, here), LANES - 1, axis=1)
        west = pltpu.roll(jnp.where(last_lane, before, here), 1, axis=1)
        return (east - west) * rows.half

    def north(here):
        return pltpu.roll(here, ROWS - 1, axis=0)

    def south(here):
        return pltpu.roll(here, 1, axis=0)

    def merid_flux(here):
        return up * north(here) - down * south(here)

    def merid_diff(here):
        return half_up * north(here) - half_down * south(here)

    def x(p, g):
        return x_ref[tile(p, g), :]

    def around(p):
        return lax.rem(p + blocks - 1, blocks), lax.rem(p + 1, blocks)

    def divergence(p, carry):
        before, after = around(p)
        for level in range(2):
            u, v = 2 + level, 4 + level
            div_ref[p, level] = zonal_diff(x(before, u), x(p, u), x(after, u)) + merid_flux(x(p, v))
        return carry

    lax.fori_loop(0, blocks, divergence, 0, unroll=blocks)

    def increments(p, carry):
        before, after = around(p)
        for level in range(2):
            h, u, v, t = level, 2 + level, 4 + level, 6 + level
            damp = damping[level]
            thick, zonal, merid, potential = x(p, h), x(p, u), x(p, v), x(p, t)
            thick_b, thick_a = x(before, h), x(after, h)
            carried = 1.0 + thick
            flux_b, flux_a = (1.0 + thick_b) * x(before, u), (1.0 + thick_a) * x(after, u)
            inc_ref[tile(p, h), :] = -COURANT * (
                zonal_diff(flux_b, carried * zonal, flux_a) + merid_flux(carried * merid)
            )
            div = div_ref[p, level]
            inc_ref[tile(p, u), :] = COURANT * (
                rows.coriolis * merid - zonal_diff(thick_b, thick, thick_a)
            ) + damp * zonal_diff(div_ref[before, level], div, div_ref[after, level])
            inc_ref[tile(p, v), :] = damp * merid_diff(div) - COURANT * (
                rows.coriolis * zonal + merid_diff(thick)
            )
            inc_ref[tile(p, t), :] = -COURANT * (
                zonal * zonal_diff(x(before, t), potential, x(after, t))
                + merid * merid_diff(potential)
            )
        return carry

    lax.fori_loop(0, blocks, increments, 0, unroll=blocks)


def filter_kernel(
    bands,
    blocks,
    x_ref,
    inc_ref,
    z_ref,
    c_ref,
    own_ref,
    param_ref,
    twist_ref,
    forward_ref,
    inverse_ref,
    out_ref,
    wave_ref,
):
    del inc_ref
    rows = Rows(bands)
    damping = [rows.square * param_ref[i] for i in range(2)]
    lane = lax.broadcasted_iota(jnp.int32, (blocks, LANES), 1)

    def shifted_diff(v):
        after = jnp.where(lane == 0, pltpu.roll(v, blocks - 1, axis=0), v)
        before = jnp.where(lane == LANES - 1, pltpu.roll(v, 1, axis=0), v)
        return pltpu.roll(after, LANES - 1, axis=1) - pltpu.roll(before, 1, axis=1)

    def add(group, row, value):
        at = pl.ds(group * ROWS + row, blocks, stride=8 * ROWS)
        out_ref[at, :] = out_ref[at, :] + value

    for side in range(2):
        edge, inner = side * (ROWS - 1), 1 + side * (ROWS - 3)
        half, up, down, inside = rows.beside(side)
        weight = rows.up[edge : edge + 1] if side else -rows.down[edge : edge + 1]
        step = 0.5 if side else -0.5
        for level in range(2):
            damp = damping[level]
            damp_edge, damp_inner = damp[edge : edge + 1], damp[inner : inner + 1]

            def beyond(k):
                other = c_ref[1 - rows.core, k * 2 + level]
                return jnp.where(rows.core == side, z_ref[k * 2 + level], other) * inside

            thick, zonal, potential, near, far = (beyond(k) for k in range(5))
            own = own_ref[side * 2 + level]
            above, below = (far, own) if side else (own, far)
            div = shifted_diff(zonal) * half + up * above - down * below
            more = weight * near
            add(level, edge, -COURANT * weight * ((1.0 + thick) * near))
            add(2 + level, edge, damp_edge * rows.half[edge : edge + 1] * shifted_diff(more))
            add(4 + level, edge, step * (damp_edge * div - COURANT * thick))
            add(4 + level, inner, step * damp_inner * more)
            add(6 + level, edge, -COURANT * step * (own * potential))

    polar = rows.polar
    limit = param_ref[2].astype(jnp.int32)
    any_polar = (rows.first < rows.nlat // 4) | (rows.first + ROWS > rows.nlat - rows.nlat // 4)
    top = blocks // 2
    nlon = blocks * LANES

    @pl.when(jnp.logical_not(any_polar))
    def _():
        out_ref[...] = x_ref[...] + out_ref[...]

    @pl.when(any_polar)
    def _():
        def analyse(g, carry):
            waves = real_fft([out_ref[tile(p, g), :] for p in range(blocks)])
            at = pl.ds(pl.multiple_of(g * ROWS, ROWS), ROWS)
            for k, (re, im) in enumerate(waves):
                c, s = twist_ref[0, k], twist_ref[1, k]
                if im is None:
                    turned = (re, jnp.zeros_like(re)) if k == 0 else (re * c, -(re * s))
                else:
                    turned = (re * c + im * s, im * c - re * s)
                wave_ref[k, at, :LANES], wave_ref[k, at, LANES:] = turned
            return carry

        lax.fori_loop(0, 8, analyse, 0, unroll=8)

        def product(values, table_ref):
            high, low = split(values)
            dot = lambda a, b: jnp.dot(a, b, preferred_element_type=jnp.float32)
            return dot(high, table_ref[0]) + dot(low, table_ref[0]) + dot(high, table_ref[1])

        def middle(start, stop):
            count = (stop - start) * 8 * ROWS
            spectrum = product(wave_ref[start:stop].reshape(count, 2 * LANES), forward_ref)
            spectrum = spectrum.reshape(stop - start, 8, ROWS, 2 * LANES)
            wave = start + lax.broadcasted_iota(jnp.int32, (stop - start, 1, ROWS, LANES), 0)
            step = lax.broadcasted_iota(jnp.int32, (stop - start, 1, ROWS, LANES), 3)
            wave = wave + blocks * step
            kept = jnp.minimum(wave, nlon - wave) <= limit
            kept = jnp.concatenate([kept, kept], axis=-1)
            spectrum = jnp.where(kept, spectrum, 0.0).reshape(count, 2 * LANES)
            smooth = product(spectrum, inverse_ref)
            wave_ref[start:stop] = smooth.reshape(stop - start, 8 * ROWS, 2 * LANES)

        edges = [i * (top + 1) // 8 for i in range(9)]
        for start, stop in zip(edges, edges[1:]):
            middle(start, stop)

        def rebuild(g, carry):
            at = pl.ds(pl.multiple_of(g * ROWS, ROWS), ROWS)
            waves = []
            for k in range(top + 1):
                re, im = wave_ref[k, at, :LANES], wave_ref[k, at, LANES:]
                c, s = twist_ref[0, k], twist_ref[1, k]
                if k == 0:
                    waves.append((re, None))
                elif k == top:
                    waves.append((re * c - im * s, None))
                else:
                    waves.append((re * c - im * s, im * c + re * s))
            for p, smooth in enumerate(real_ifft(waves)):
                here = tile(p, g)
                out_ref[here, :] = x_ref[here, :] + jnp.where(polar, smooth, out_ref[here, :])
            return carry

        lax.fori_loop(0, 8, rebuild, 0, unroll=8)


def on_device(state, damping, cutoff):
    fields, levels, nrow, ncol = state.shape
    bands, blocks = lax.axis_size("lat"), lax.axis_size("lon")
    chips = blocks // 2
    vmem, hbm = pl.BlockSpec(memory_space=pltpu.VMEM), pl.BlockSpec(memory_space=pltpu.HBM)
    limits = pltpu.CompilerParams(vmem_limit_bytes=40 * 2**20)

    def call(kernel, name, out, ins, outs, cost, scratch=(), aliases=None):
        return pl.pallas_call(
            kernel,
            out_shape=out,
            in_specs=ins,
            out_specs=outs,
            scratch_shapes=scratch,
            compiler_params=limits,
            input_output_aliases=aliases or {},
            cost_estimate=pl.CostEstimate(flops=cost, bytes_accessed=2**22, transcendentals=0),
            name=name,
        )

    def array(*shape):
        return jax.ShapeDtypeStruct(shape, jnp.float32)

    sems = [pltpu.SemaphoreType.DMA((fields, 2))]
    parts = call(
        spread_kernel, "spread", array(chips, 2, fields, 2, ROWS, ncol), [hbm], vmem, 0, sems
    )(state.reshape(fields, chips, 2, 2, ROWS, ncol))
    circles = lax.all_to_all(
        parts.reshape(blocks, -1, ncol), "lon", split_axis=0, concat_axis=0, tiled=True
    ).reshape(-1, ncol)

    twist, forward, inverse = fourier_tables(blocks)

    plane = array(10, blocks, ncol)
    z_mine, c_mine, own = call(
        lambda *refs: pack_kernel(blocks, *refs),
        "pack",
        (plane, plane, array(4, blocks, ncol)),
        [vmem],
        (vmem, vmem, vmem),
        0,
    )(circles)

    swaps = []
    for z in range(bands - 1):
        for m in range(chips):
            a, b = z * blocks + 2 * m + 1, (z + 1) * blocks + 2 * m
            swaps += [(a, b), (b, a)]
    z_other = lax.ppermute(z_mine, ("lat", "lon"), swaps)
    pairs = [[2 * m, 2 * m + 1] for m in range(chips)]
    c_both = lax.all_gather(c_mine, "lon", axis_index_groups=pairs)
    increments, params = call(
        lambda *refs: stencil_kernel(bands, blocks, *refs),
        "stencil",
        (array(*circles.shape), array(3, ROWS, ncol)),
        [vmem] * 3,
        (vmem, vmem),
        2**31,
        [pltpu.VMEM((blocks, 2, ROWS, ncol), jnp.float32)],
    )(circles, damping, cutoff)
    moved = call(
        lambda *refs: filter_kernel(bands, blocks, *refs),
        "filter",
        array(*circles.shape),
        [vmem] * 9,
        vmem,
        2**31,
        [pltpu.VMEM((blocks // 2 + 1, 8 * ROWS, 2 * ncol), jnp.float32)],
        {1: 0},
    )(circles, increments, z_other, c_both, own, params, twist, forward, inverse)

    home = lax.all_to_all(
        moved.reshape(blocks, -1, ncol), "lon", split_axis=0, concat_axis=0, tiled=True
    )
    out = call(
        collect_kernel, "collect", array(fields, chips, 2, 2, ROWS, ncol), [vmem], hbm, 0, sems
    )(home.reshape(chips, 2, fields, 2, ROWS, ncol))
    return out.reshape(state.shape)


def solution(mesh):
    in_specs = (P(None, None, "lat", "lon"), P(), P())
    out_specs = P(None, None, "lat", "lon")
    return jax.shard_map(
        on_device, mesh=mesh, in_specs=in_specs, out_specs=out_specs, check_vma=False
    )
```

```python
import math

import jax
import jax.numpy as jnp
import numpy as np
from jax import lax
from jax.experimental import pallas as pl
from jax.experimental.pallas import tpu as pltpu
from jax.sharding import PartitionSpec as P

COURANT = 0.05
ROWS = 8
LANES = 128


def sine(angle):
    square = angle * angle
    total = jnp.zeros_like(angle)
    for n in (13, 11, 9, 7, 5, 3, 1):
        total = total * square + (-1.0) ** (n // 2) / math.factorial(n)
    return total * angle


class Rows:
    def __init__(self, bands):
        self.core = lax.axis_index("lon") % 2
        self.first = (lax.axis_index("lat") * 2 + self.core) * ROWS
        self.nlat = nlat = bands * 2 * ROWS
        row = lax.broadcasted_iota(jnp.int32, (ROWS, LANES), 0)
        near = self.first + row
        at = self.cosine(near)
        self.half = 0.5 / at
        self.up, self.down = self.cosine(near + 1) * self.half, self.cosine(near - 1) * self.half
        middle = near.astype(jnp.float32) + (0.5 - 0.5 * nlat)
        self.coriolis = 2.0 * sine(middle * (math.pi / nlat))
        self.square = at * at
        self.polar = (near < nlat // 4) | (near >= nlat - nlat // 4)
        ends = self.first + jnp.where(row < 3, row - 2, row + ROWS - 4)
        self.ends = self.cosine(ends)

    def cosine(self, row):
        index = row.astype(jnp.float32) + 0.5
        return sine(jnp.minimum(index, self.nlat - index) * (math.pi / self.nlat))

    def beside(self, side):
        below, at, above = (self.ends[side * 3 + i : side * 3 + i + 1] for i in range(3))
        row = self.first + (ROWS if side else -1)
        inside = ((row >= 0) & (row < self.nlat)).astype(jnp.float32)
        half = 0.5 / at * inside
        return (-below if side else above) * half, inside


def split(values):
    high = values.astype(jnp.bfloat16)
    low = (values - high.astype(jnp.float32)).astype(jnp.bfloat16)
    return high, low


def fourier_tables(blocks):
    nlon = blocks * LANES
    at = np.arange(LANES)
    phase = 2.0 * np.pi * ((at[:, None] * at[None, :]) % LANES) / LANES
    cos, sin = np.cos(phase), np.sin(phase)
    forward = np.block([[cos, -sin], [sin, cos]])
    inverse = np.block([[cos, sin], [-sin, cos]]) / nlon
    turn = 2.0 * np.pi * np.arange(blocks // 2 + 1)[:, None] * at[None, :] / nlon
    twist = np.stack([np.cos(turn), np.sin(turn)]).astype(np.float32)
    twist = np.broadcast_to(twist[:, :, None, :], (2, blocks // 2 + 1, ROWS, LANES))

    def halves(matrix):
        high = matrix.astype(np.float32).astype(jnp.bfloat16)
        low = (matrix - high.astype(np.float64)).astype(np.float32).astype(jnp.bfloat16)
        return np.stack([high, low])

    return np.ascontiguousarray(twist), halves(forward), halves(inverse)


def root(k, n):
    angle = 2.0 * math.pi * k / n
    return math.cos(angle), math.sin(angle)


def real_fft(x):
    n = len(x)
    if n == 2:
        return [(x[0] + x[1], None), (x[0] - x[1], None)]
    even, odd = real_fft(x[0::2]), real_fft(x[1::2])
    half, quarter = n // 2, n // 4
    out = [None] * (half + 1)
    out[0] = (even[0][0] + odd[0][0], None)
    out[half] = (even[0][0] - odd[0][0], None)
    out[quarter] = (even[quarter][0], -odd[quarter][0])
    for k in range(1, quarter):
        c, s = root(k, n)
        re, im = odd[k]
        t_re, t_im = re * c + im * s, im * c - re * s
        out[k] = (even[k][0] + t_re, even[k][1] + t_im)
        out[half - k] = (even[k][0] - t_re, t_im - even[k][1])
    return out


def real_ifft(w):
    half = len(w) - 1
    n, quarter = 2 * half, half // 2
    if n == 2:
        return [w[0][0] + w[1][0], w[0][0] - w[1][0]]
    even, odd = [None] * (quarter + 1), [None] * (quarter + 1)
    even[0] = (w[0][0] + w[half][0], None)
    odd[0] = (w[0][0] - w[half][0], None)
    even[quarter] = (2.0 * w[quarter][0], None)
    odd[quarter] = (-2.0 * w[quarter][1], None)
    for k in range(1, quarter):
        c, s = root(k, n)
        a, b = w[k], w[half - k]
        even[k] = (a[0] + b[0], a[1] - b[1])
        re, im = a[0] - b[0], a[1] + b[1]
        odd[k] = (re * c - im * s, im * c + re * s)
    x = [None] * n
    x[0::2], x[1::2] = real_ifft(even), real_ifft(odd)
    return x


def spread_kernel(x_ref, out_ref, sems):
    copies = []
    for field in range(4):
        for core in range(2):
            copies.append(
                pltpu.make_async_copy(
                    x_ref.at[field, :, :, core], out_ref.at[:, core, field], sems.at[field, core]
                )
            )
    for copy in copies:
        copy.start()
    for copy in copies:
        copy.wait()


def collect_kernel(x_ref, out_ref, sems):
    copies = []
    for field in range(4):
        for core in range(2):
            copies.append(
                pltpu.make_async_copy(
                    x_ref.at[:, core, field], out_ref.at[field, :, :, core], sems.at[field, core]
                )
            )
    for copy in copies:
        copy.start()
    for copy in copies:
        copy.wait()


def shifted_diff(here):
    blocks = here.shape[0]
    lane = lax.broadcasted_iota(jnp.int32, here.shape, 1)
    after = jnp.where(lane == 0, pltpu.roll(here, blocks - 1, axis=0), here)
    before = jnp.where(lane == LANES - 1, pltpu.roll(here, 1, axis=0), here)
    return pltpu.roll(after, LANES - 1, axis=1) - pltpu.roll(before, 1, axis=1)


def pack_kernel(bands, blocks, x_ref, z_ref, c_ref, own_ref):
    rows = Rows(bands)

    def plane(field, level, row):
        return x_ref[pl.ds((field * 2 + level) * ROWS + row, blocks, stride=8 * ROWS), :]

    for out, end in ((z_ref, rows.core), (c_ref, 1 - rows.core)):
        edge, inner = end * (ROWS - 1), 1 + end * (ROWS - 3)
        half, weight = (
            jnp.where(end == 1, v[ROWS - 1 :], w[:1])
            for v, w in ((rows.half, rows.half), (-rows.down, rows.up))
        )
        for level in range(2):
            for k, field in enumerate((0, 2, 3)):
                out[k * 2 + level] = plane(field, level, edge)
            zonal, far = plane(1, level, edge), plane(2, level, inner)
            out[6 + level] = shifted_diff(zonal) * half + weight * far
    for side in range(2):
        for level in range(2):
            own_ref[side * 2 + level] = plane(2, level, side * (ROWS - 1))


def parameters(rows, damp_ref, cutoff_ref, param_ref):
    level = lax.axis_index("lon") // 2 * 2
    damping = damp_ref[...].reshape(1, -1)
    at = lax.broadcasted_iota(jnp.int32, damping.shape, 1)
    for i in range(2):
        one = jnp.sum(jnp.where(at == level + i, damping, 0.0), axis=1, keepdims=True)
        param_ref[i] = jnp.broadcast_to(one, (ROWS, LANES))
    cutoff = cutoff_ref[...].astype(jnp.float32).reshape(1, -1)
    cutoff = jnp.broadcast_to(cutoff, (ROWS, cutoff.shape[1]))
    at = lax.broadcasted_iota(jnp.int32, cutoff.shape, 1)
    row = lax.broadcasted_iota(jnp.int32, cutoff.shape, 0)
    limit = jnp.sum(jnp.where(at == rows.first + row, cutoff, 0.0), axis=1, keepdims=True)
    param_ref[2] = jnp.broadcast_to(limit, (ROWS, LANES))


def tile(p, g):
    start = (p * 8 + g) * ROWS
    return pl.ds(start if isinstance(start, int) else pl.multiple_of(start, ROWS), ROWS)


def stencil_kernel(bands, blocks, x_ref, damp_ref, cutoff_ref, inc_ref, param_ref, mix_ref):
    rows = Rows(bands)
    parameters(rows, damp_ref, cutoff_ref, param_ref)
    row = lax.broadcasted_iota(jnp.int32, (ROWS, LANES), 0)
    up = jnp.where(row == ROWS - 1, 0.0, rows.up)
    down = jnp.where(row == 0, 0.0, rows.down)
    half_up = jnp.where(row == ROWS - 1, 0.0, 0.5)
    half_down = jnp.where(row == 0, 0.0, 0.5)
    damping = [rows.square * param_ref[i] for i in range(2)]
    lane = lax.broadcasted_iota(jnp.int32, (ROWS, LANES), 1)
    first_lane, last_lane = lane == 0, lane == LANES - 1

    def zonal_diff(before, here, after):
        east = pltpu.roll(jnp.where(first_lane, after, here), LANES - 1, axis=1)
        west = pltpu.roll(jnp.where(last_lane, before, here), 1, axis=1)
        return (east - west) * rows.half

    def north(here):
        return pltpu.roll(here, ROWS - 1, axis=0)

    def south(here):
        return pltpu.roll(here, 1, axis=0)

    def x(p, g):
        return x_ref[tile(p, g), :]

    def around(p):
        return lax.rem(p + blocks - 1, blocks), lax.rem(p + 1, blocks)

    damping_north = [south(v) for v in damping]
    damping_south = [north(v) for v in damping]

    def first_pass(p, carry):
        before, after = around(p)
        for level in range(2):
            h, u, v = level, 2 + level, 4 + level
            thick, zonal = COURANT * x(p, h), x(p, u)
            div = zonal_diff(x(before, u), zonal, x(after, u))
            div = div + up * north(x(p, v)) - down * south(x(p, v))
            mix_ref[p, level] = damping[level] * div - thick
            rise = half_up * north(damping_north[level] * div - thick)
            rise = rise - half_down * south(damping_south[level] * div - thick)
            inc_ref[tile(p, v), :] = rise - COURANT * (rows.coriolis * zonal)
        return carry

    lax.fori_loop(0, blocks, first_pass, 0, unroll=blocks)

    def second_pass(p, carry):
        before, after = around(p)
        for level in range(2):
            h, u, v, t = level, 2 + level, 4 + level, 6 + level
            zonal, merid, potential = x(p, u), x(p, v), x(p, t)
            carried = 1.0 + x(p, h)
            flux_b, flux_a = (1.0 + x(before, h)) * x(before, u), (1.0 + x(after, h)) * x(after, u)
            flow = carried * merid
            inc_ref[tile(p, h), :] = -COURANT * (
                zonal_diff(flux_b, carried * zonal, flux_a) + up * north(flow) - down * south(flow)
            )
            inc_ref[tile(p, u), :] = COURANT * (rows.coriolis * merid) + zonal_diff(
                mix_ref[before, level], mix_ref[p, level], mix_ref[after, level]
            )
            rise = half_up * north(potential) - half_down * south(potential)
            inc_ref[tile(p, t), :] = -COURANT * (
                zonal * zonal_diff(x(before, t), potential, x(after, t)) + merid * rise
            )
        return carry

    lax.fori_loop(0, blocks, second_pass, 0, unroll=blocks)


def filter_kernel(
    bands,
    blocks,
    x_ref,
    inc_ref,
    z_ref,
    c_ref,
    own_ref,
    param_ref,
    twist_ref,
    forward_ref,
    inverse_ref,
    out_ref,
    more_ref,
    wave_ref,
):
    rows = Rows(bands)
    damping = [rows.square * param_ref[i] for i in range(2)]
    for side in range(2):
        edge, inner = side * (ROWS - 1), 1 + side * (ROWS - 3)
        across, inside = rows.beside(side)
        weight = rows.up[edge : edge + 1] if side else -rows.down[edge : edge + 1]
        step = 0.5 if side else -0.5
        for level in range(2):
            damp = damping[level]
            damp_edge, damp_inner = damp[edge : edge + 1], damp[inner : inner + 1]

            def beyond(k):
                other = c_ref[1 - rows.core, k * 2 + level]
                return jnp.where(rows.core == side, z_ref[k * 2 + level], other) * inside

            thick, near, potential, div = (beyond(k) for k in range(4))
            own = own_ref[side * 2 + level]
            div = div + across * own
            extra = weight * near
            more_ref[side, level] = -COURANT * weight * ((1.0 + thick) * near)
            more_ref[side, 2 + level] = damp_edge * rows.half[edge : edge + 1] * shifted_diff(extra)
            more_ref[side, 4 + level] = step * (damp_edge * div - COURANT * thick)
            more_ref[side, 6 + level] = -COURANT * step * (own * potential)
            more_ref[side, 8 + level] = step * damp_inner * extra

    row = lax.broadcasted_iota(jnp.int32, (ROWS, LANES), 0)

    def increment(p, g):
        def more(side, k):
            return more_ref[side, k, p : p + 1, :]

        total = jnp.where(row == 0, more(0, g), jnp.where(row == ROWS - 1, more(1, g), 0.0))
        if g // 2 == 2:
            total = jnp.where(row == 1, more(0, g + 4), total)
            total = jnp.where(row == ROWS - 2, more(1, g + 4), total)
        return inc_ref[tile(p, g), :] + total

    limit = param_ref[2].astype(jnp.int32)
    any_polar = (rows.first < rows.nlat // 4) | (rows.first + ROWS > rows.nlat - rows.nlat // 4)
    whole = rows.nlat // 4 % ROWS == 0
    top = blocks // 2
    nlon = blocks * LANES

    @pl.when(jnp.logical_not(any_polar))
    def _():
        for g in range(8):
            for p in range(blocks):
                out_ref[tile(p, g), :] = x_ref[tile(p, g), :] + increment(p, g)

    @pl.when(any_polar)
    def _():
        width = 2

        def analyse(part):
            for i in range(width):
                waves = real_fft([increment(p, part * width + i) for p in range(blocks)])
                at = slice(i * ROWS, (i + 1) * ROWS)
                for k, (re, im) in enumerate(waves):
                    c, s = twist_ref[0, k], twist_ref[1, k]
                    if im is None:
                        turned = (re, jnp.zeros_like(re)) if k == 0 else (re * c, -(re * s))
                    else:
                        turned = (re * c + im * s, im * c - re * s)
                    wave_ref[part, k, at, :LANES], wave_ref[part, k, at, LANES:] = turned

        def product(values, table_ref):
            high, low = split(values)
            dot = lambda a, b: jnp.dot(a, b, preferred_element_type=jnp.float32)
            return dot(low, table_ref[0]) + dot(high, table_ref[0]) + dot(high, table_ref[1])

        wave = lax.broadcasted_iota(jnp.int32, (top + 1, 1, ROWS, LANES), 0)
        wave = wave + blocks * lax.broadcasted_iota(jnp.int32, (top + 1, 1, ROWS, LANES), 3)
        kept = jnp.minimum(wave, nlon - wave) <= limit
        kept = jnp.concatenate([kept, kept], axis=-1)

        def middle(part):
            count = (top + 1) * width * ROWS
            spectrum = product(wave_ref[part].reshape(count, 2 * LANES), forward_ref)
            spectrum = spectrum.reshape(top + 1, width, ROWS, 2 * LANES)
            spectrum = jnp.where(kept, spectrum, 0.0).reshape(count, 2 * LANES)
            smooth = product(spectrum, inverse_ref)
            wave_ref[part] = smooth.reshape(top + 1, width * ROWS, 2 * LANES)

        def rebuild(part):
            for i in range(width):
                g = part * width + i
                at = slice(i * ROWS, (i + 1) * ROWS)
                waves = []
                for k in range(top + 1):
                    re, im = wave_ref[part, k, at, :LANES], wave_ref[part, k, at, LANES:]
                    c, s = twist_ref[0, k], twist_ref[1, k]
                    if k == 0:
                        waves.append((re, None))
                    elif k == top:
                        waves.append((re * c - im * s, None))
                    else:
                        waves.append((re * c - im * s, im * c + re * s))
                for p, smooth in enumerate(real_ifft(waves)):
                    if not whole:
                        smooth = jnp.where(rows.polar, smooth, increment(p, g))
                    out_ref[tile(p, g), :] = x_ref[tile(p, g), :] + smooth

        parts = 8 // width
        for i in range(parts + 2):
            if i < parts:
                analyse(i)
            if 1 <= i <= parts:
                middle(i - 1)
            if i >= 2:
                rebuild(i - 2)


def on_device(state, damping, cutoff):
    fields, levels, nrow, ncol = state.shape
    bands, blocks = lax.axis_size("lat"), lax.axis_size("lon")
    chips = blocks // 2
    vmem, hbm = pl.BlockSpec(memory_space=pltpu.VMEM), pl.BlockSpec(memory_space=pltpu.HBM)
    limits = pltpu.CompilerParams(vmem_limit_bytes=40 * 2**20)

    def call(kernel, name, out, ins, outs, cost, scratch=()):
        return pl.pallas_call(
            kernel,
            out_shape=out,
            in_specs=ins,
            out_specs=outs,
            scratch_shapes=scratch,
            compiler_params=limits,
            cost_estimate=pl.CostEstimate(flops=cost, bytes_accessed=2**22, transcendentals=0),
            name=name,
        )

    def array(*shape):
        return jax.ShapeDtypeStruct(shape, jnp.float32)

    sems = [pltpu.SemaphoreType.DMA((fields, 2))]
    parts = call(
        spread_kernel, "spread", array(chips, 2, fields, 2, ROWS, ncol), [hbm], vmem, 0, sems
    )(state.reshape(fields, chips, 2, 2, ROWS, ncol))
    circles = lax.all_to_all(
        parts.reshape(blocks, -1, ncol), "lon", split_axis=0, concat_axis=0, tiled=True
    ).reshape(-1, ncol)

    twist, forward, inverse = fourier_tables(blocks)

    plane = array(8, blocks, ncol)
    z_mine, c_mine, own = call(
        lambda *refs: pack_kernel(bands, blocks, *refs),
        "pack",
        (plane, plane, array(4, blocks, ncol)),
        [vmem],
        (vmem, vmem, vmem),
        0,
    )(circles)

    swaps = []
    for z in range(bands - 1):
        for m in range(chips):
            a, b = z * blocks + 2 * m + 1, (z + 1) * blocks + 2 * m
            swaps += [(a, b), (b, a)]
    z_other = lax.ppermute(z_mine, ("lat", "lon"), swaps)
    pairs = [[2 * m, 2 * m + 1] for m in range(chips)]
    c_both = lax.all_gather(c_mine, "lon", axis_index_groups=pairs)
    increments, params = call(
        lambda *refs: stencil_kernel(bands, blocks, *refs),
        "stencil",
        (array(*circles.shape), array(3, ROWS, ncol)),
        [vmem] * 3,
        (vmem, vmem),
        2**28,
        [pltpu.VMEM((blocks, 2, ROWS, ncol), jnp.float32)],
    )(circles, damping, cutoff)
    moved = call(
        lambda *refs: filter_kernel(bands, blocks, *refs),
        "filter",
        array(*circles.shape),
        [vmem] * 9,
        vmem,
        2**31,
        [
            pltpu.VMEM((2, 10, blocks, ncol), jnp.float32),
            pltpu.VMEM((4, blocks // 2 + 1, 2 * ROWS, 2 * ncol), jnp.float32),
        ],
    )(circles, increments, z_other, c_both, own, params, twist, forward, inverse)

    home = lax.all_to_all(
        moved.reshape(blocks, -1, ncol), "lon", split_axis=0, concat_axis=0, tiled=True
    )
    out = call(
        collect_kernel, "collect", array(fields, chips, 2, 2, ROWS, ncol), [vmem], hbm, 0, sems
    )(home.reshape(chips, 2, fields, 2, ROWS, ncol))
    return out.reshape(state.shape)


def solution(mesh):
    in_specs = (P(None, None, "lat", "lon"), P(), P())
    out_specs = P(None, None, "lat", "lon")
    return jax.shard_map(
        on_device, mesh=mesh, in_specs=in_specs, out_specs=out_specs, check_vma=False
    )
```

```python
import math

import jax
import jax.numpy as jnp
import numpy as np
from jax import lax
from jax.experimental import pallas as pl
from jax.experimental.pallas import tpu as pltpu
from jax.sharding import PartitionSpec as P

COURANT = 0.05
ROWS = 8
LANES = 128


def sine(angle):
    square = angle * angle
    total = jnp.zeros_like(angle)
    for n in (13, 11, 9, 7, 5, 3, 1):
        total = total * square + (-1.0) ** (n // 2) / math.factorial(n)
    return total * angle


class Rows:
    def __init__(self, bands):
        self.core = lax.axis_index("lon") % 2
        self.first = (lax.axis_index("lat") * 2 + self.core) * ROWS
        self.nlat = nlat = bands * 2 * ROWS
        row = lax.broadcasted_iota(jnp.int32, (ROWS, LANES), 0)
        near = self.first + row
        at = self.cosine(near)
        self.half = 0.5 / at
        self.up, self.down = self.cosine(near + 1) * self.half, self.cosine(near - 1) * self.half
        middle = near.astype(jnp.float32) + (0.5 - 0.5 * nlat)
        self.coriolis = 2.0 * sine(middle * (math.pi / nlat))
        self.square = at * at
        self.polar = (near < nlat // 4) | (near >= nlat - nlat // 4)
        ends = self.first + jnp.where(row < 3, row - 2, row + ROWS - 4)
        self.ends = self.cosine(ends)

    def cosine(self, row):
        index = row.astype(jnp.float32) + 0.5
        return sine(jnp.minimum(index, self.nlat - index) * (math.pi / self.nlat))

    def beside(self, side):
        below, at, above = (self.ends[side * 3 + i : side * 3 + i + 1] for i in range(3))
        row = self.first + (ROWS if side else -1)
        inside = ((row >= 0) & (row < self.nlat)).astype(jnp.float32)
        half = 0.5 / at * inside
        return (-below if side else above) * half, inside


def split(values):
    high = values.astype(jnp.bfloat16)
    low = (values - high.astype(jnp.float32)).astype(jnp.bfloat16)
    return high, low


def fourier_tables(blocks):
    nlon = blocks * LANES
    at = np.arange(LANES)
    phase = 2.0 * np.pi * ((at[:, None] * at[None, :]) % LANES) / LANES
    cos, sin = np.cos(phase), np.sin(phase)
    forward = np.block([[cos, -sin], [sin, cos]])
    inverse = np.block([[cos, sin], [-sin, cos]]) / nlon
    angle = 2.0 * np.pi * np.arange(blocks // 2 + 1)[:, None] * at[None, :] / nlon
    twice = np.where(np.arange(blocks // 2 + 1) % (blocks // 2) == 0, 1.0, math.sqrt(2.0))[:, None]
    twist = np.stack([twice * np.cos(angle), twice * np.sin(angle)]).astype(np.float32)
    twist = np.broadcast_to(twist[:, :, None, :], (2, blocks // 2 + 1, ROWS, LANES))

    def halves(matrix):
        high = matrix.astype(np.float32).astype(jnp.bfloat16)
        low = (matrix - high.astype(np.float64)).astype(np.float32).astype(jnp.bfloat16)
        return np.stack([high, low])

    return np.ascontiguousarray(twist), halves(forward), halves(inverse)


class Signed:
    def __init__(self, value, minus=False):
        self.value, self.minus = value, minus

    def __neg__(self):
        return Signed(self.value, not self.minus)

    def __add__(self, other):
        if self.minus == other.minus:
            return Signed(self.value + other.value, self.minus)
        first, second = (other, self) if self.minus else (self, other)
        return Signed(first.value - second.value)

    def __sub__(self, other):
        return self + -other

    def __mul__(self, factor):
        return Signed(self.value * factor, self.minus)

    def plain(self):
        return -self.value if self.minus else self.value


def turn(re, im, k, n):
    if 8 * k == n:
        c = math.sqrt(0.5)
        return (re + im) * c, (im - re) * c
    angle = 2.0 * math.pi * k / n
    c, s = math.cos(angle), math.sin(angle)
    return re * c + im * s, im * c - re * s


def real_fft(x):
    n = len(x)
    if n == 2:
        return [(x[0] + x[1], None), (x[0] - x[1], None)]
    even, odd = real_fft(x[0::2]), real_fft(x[1::2])
    half, quarter = n // 2, n // 4
    out = [None] * (half + 1)
    out[0] = (even[0][0] + odd[0][0], None)
    out[half] = (even[0][0] - odd[0][0], None)
    out[quarter] = (even[quarter][0], -odd[quarter][0])
    for k in range(1, quarter):
        re, im = turn(*odd[k], k, n)
        out[k] = (even[k][0] + re, even[k][1] + im)
        out[half - k] = (even[k][0] - re, im - even[k][1])
    return out


def real_ifft(w):
    half = len(w) - 1
    n, quarter = 2 * half, half // 2
    if n == 2:
        return [w[0][0] + w[1][0], w[0][0] - w[1][0]]
    even, odd = [None] * (quarter + 1), [None] * (quarter + 1)
    even[0] = (w[0][0] + w[half][0], None)
    odd[0] = (w[0][0] - w[half][0], None)
    even[quarter] = (w[quarter][0], None)
    odd[quarter] = (-w[quarter][1], None)
    for k in range(1, quarter):
        a, b = w[k], w[half - k]
        even[k] = (a[0] + b[0], a[1] - b[1])
        im, re = turn(a[1] + b[1], a[0] - b[0], k, n)
        odd[k] = (re, im)
    x = [None] * n
    x[0::2], x[1::2] = real_ifft(even), real_ifft(odd)
    return x


def spread_kernel(x_ref, out_ref, sems):
    copies = []
    for field in range(4):
        for core in range(2):
            copies.append(
                pltpu.make_async_copy(
                    x_ref.at[field, :, :, core], out_ref.at[:, core, field], sems.at[field, core]
                )
            )
    for copy in copies:
        copy.start()
    for copy in copies:
        copy.wait()


def collect_kernel(x_ref, out_ref, sems):
    copies = []
    for field in range(4):
        for core in range(2):
            copies.append(
                pltpu.make_async_copy(
                    x_ref.at[:, core, field], out_ref.at[field, :, :, core], sems.at[field, core]
                )
            )
    for copy in copies:
        copy.start()
    for copy in copies:
        copy.wait()


def shifted_diff(here):
    blocks = here.shape[0]
    lane = lax.broadcasted_iota(jnp.int32, here.shape, 1)
    after = jnp.where(lane == 0, pltpu.roll(here, blocks - 1, axis=0), here)
    before = jnp.where(lane == LANES - 1, pltpu.roll(here, 1, axis=0), here)
    return pltpu.roll(after, LANES - 1, axis=1) - pltpu.roll(before, 1, axis=1)


def pack(rows, end, x_ref, out_ref):
    edge, inner = end * (ROWS - 1), 1 + end * (ROWS - 3)
    last = end == 1
    half = jnp.where(last, rows.half[ROWS - 1 :], rows.half[:1])
    weight = jnp.where(last, -rows.down[ROWS - 1 :], rows.up[:1])
    for level in range(2):

        def plane(field, row):
            return x_ref[:, (field * 2 + level) * ROWS + row, :]

        for k, field in enumerate((0, 2, 3)):
            out_ref[k * 2 + level] = plane(field, edge)
        out_ref[6 + level] = shifted_diff(plane(1, edge)) * half + weight * plane(2, inner)


def pack_kernel(bands, x_ref, z_ref):
    rows = Rows(bands)
    pack(rows, rows.core, x_ref, z_ref)


def parameters(rows, damp_ref, cutoff_ref, param_ref):
    level = lax.axis_index("lon") // 2 * 2
    damping = damp_ref[...].reshape(1, -1)
    at = lax.broadcasted_iota(jnp.int32, damping.shape, 1)
    for i in range(2):
        one = jnp.sum(jnp.where(at == level + i, damping, 0.0), axis=1, keepdims=True)
        param_ref[i] = jnp.broadcast_to(one, (ROWS, LANES))
    cutoff = cutoff_ref[...].astype(jnp.float32).reshape(1, -1)
    cutoff = jnp.broadcast_to(cutoff, (ROWS, cutoff.shape[1]))
    at = lax.broadcasted_iota(jnp.int32, cutoff.shape, 1)
    row = lax.broadcasted_iota(jnp.int32, cutoff.shape, 0)
    limit = jnp.sum(jnp.where(at == rows.first + row, cutoff, 0.0), axis=1, keepdims=True)
    param_ref[2] = jnp.broadcast_to(limit, (ROWS, LANES))


def tile(p, g):
    start = (p * 8 + g) * ROWS
    return pl.ds(start if isinstance(start, int) else pl.multiple_of(start, ROWS), ROWS)


def stencil_kernel(
    bands, blocks, x_ref, damp_ref, cutoff_ref, inc_ref, param_ref, c_ref, own_ref, mix_ref
):
    rows = Rows(bands)
    parameters(rows, damp_ref, cutoff_ref, param_ref)
    pack(rows, 1 - rows.core, x_ref, c_ref)
    for side in range(2):
        for level in range(2):
            own_ref[side * 2 + level] = x_ref[:, (4 + level) * ROWS + side * (ROWS - 1), :]
    row = lax.broadcasted_iota(jnp.int32, (ROWS, LANES), 0)
    up = jnp.where(row == ROWS - 1, 0.0, rows.up)
    down = jnp.where(row == 0, 0.0, rows.down)
    half_up = jnp.where(row == ROWS - 1, 0.0, 0.5)
    half_down = jnp.where(row == 0, 0.0, 0.5)
    damping = [rows.square * param_ref[i] for i in range(2)]
    lane = lax.broadcasted_iota(jnp.int32, (ROWS, LANES), 1)
    first_lane, last_lane = lane == 0, lane == LANES - 1

    def zonal_diff(before, here, after):
        east = pltpu.roll(jnp.where(first_lane, after, here), LANES - 1, axis=1)
        west = pltpu.roll(jnp.where(last_lane, before, here), 1, axis=1)
        return (east - west) * rows.half

    def north(here):
        return pltpu.roll(here, ROWS - 1, axis=0)

    def south(here):
        return pltpu.roll(here, 1, axis=0)

    def x(p, g):
        return x_ref[p, pl.ds(g * ROWS, ROWS), :]

    def around(p):
        return lax.rem(p + blocks - 1, blocks), lax.rem(p + 1, blocks)

    damping_north = [south(v) for v in damping]
    damping_south = [north(v) for v in damping]

    def first_pass(p, carry):
        before, after = around(p)
        for level in range(2):
            h, u, v = level, 2 + level, 4 + level
            thick, zonal = COURANT * x(p, h), x(p, u)
            div = zonal_diff(x(before, u), zonal, x(after, u))
            div = div + up * north(x(p, v)) - down * south(x(p, v))
            mix_ref[p, level] = damping[level] * div - thick
            rise = half_up * north(damping_north[level] * div - thick)
            rise = rise - half_down * south(damping_south[level] * div - thick)
            inc_ref[tile(p, v), :] = rise - COURANT * (rows.coriolis * zonal)
        return carry

    lax.fori_loop(0, blocks, first_pass, 0, unroll=blocks)

    def second_pass(p, carry):
        before, after = around(p)
        for level in range(2):
            h, u, v, t = level, 2 + level, 4 + level, 6 + level
            zonal, merid, potential = x(p, u), x(p, v), x(p, t)
            carried = 1.0 + x(p, h)
            flux_b, flux_a = (1.0 + x(before, h)) * x(before, u), (1.0 + x(after, h)) * x(after, u)
            flow = carried * merid
            inc_ref[tile(p, h), :] = -COURANT * (
                zonal_diff(flux_b, carried * zonal, flux_a) + up * north(flow) - down * south(flow)
            )
            inc_ref[tile(p, u), :] = COURANT * (rows.coriolis * merid) + zonal_diff(
                mix_ref[before, level], mix_ref[p, level], mix_ref[after, level]
            )
            rise = half_up * north(potential) - half_down * south(potential)
            inc_ref[tile(p, t), :] = -COURANT * (
                zonal * zonal_diff(x(before, t), potential, x(after, t)) + merid * rise
            )
        return carry

    lax.fori_loop(0, blocks, second_pass, 0, unroll=blocks)


def filter_kernel(
    bands,
    blocks,
    x_ref,
    inc_ref,
    z_ref,
    c_ref,
    own_ref,
    param_ref,
    twist_ref,
    forward_ref,
    inverse_ref,
    out_ref,
    more_ref,
    wave_ref,
):
    rows = Rows(bands)
    damping = [rows.square * param_ref[i] for i in range(2)]
    for side in range(2):
        edge, inner = side * (ROWS - 1), 1 + side * (ROWS - 3)
        across, inside = rows.beside(side)
        weight = rows.up[edge : edge + 1] if side else -rows.down[edge : edge + 1]
        step = 0.5 if side else -0.5
        for level in range(2):
            damp = damping[level]
            damp_edge, damp_inner = damp[edge : edge + 1], damp[inner : inner + 1]

            def beyond(k):
                other = c_ref[1 - rows.core, k * 2 + level]
                return jnp.where(rows.core == side, z_ref[k * 2 + level], other) * inside

            thick, near, potential, div = (beyond(k) for k in range(4))
            own = own_ref[side * 2 + level]
            div = div + across * own
            extra = weight * near
            more_ref[side, level] = -COURANT * weight * ((1.0 + thick) * near)
            more_ref[side, 2 + level] = damp_edge * rows.half[edge : edge + 1] * shifted_diff(extra)
            more_ref[side, 4 + level] = step * (damp_edge * div - COURANT * thick)
            more_ref[side, 6 + level] = -COURANT * step * (own * potential)
            more_ref[side, 8 + level] = step * damp_inner * extra

    row = lax.broadcasted_iota(jnp.int32, (ROWS, LANES), 0)

    def increment(p, g):
        def more(side, k):
            return more_ref[side, k, p : p + 1, :]

        total = jnp.where(row == 0, more(0, g), jnp.where(row == ROWS - 1, more(1, g), 0.0))
        if g // 2 == 2:
            total = jnp.where(row == 1, more(0, g + 4), total)
            total = jnp.where(row == ROWS - 2, more(1, g + 4), total)
        return inc_ref[tile(p, g), :] + total

    limit = param_ref[2].astype(jnp.int32)
    any_polar = (rows.first < rows.nlat // 4) | (rows.first + ROWS > rows.nlat - rows.nlat // 4)
    whole = rows.nlat // 4 % ROWS == 0
    top = blocks // 2
    nlon = blocks * LANES

    @pl.when(jnp.logical_not(any_polar))
    def _():
        for g in range(8):
            for p in range(blocks):
                out_ref[tile(p, g), :] = x_ref[tile(p, g), :] + increment(p, g)

    @pl.when(any_polar)
    def _():
        width = 2

        def analyse(part):
            for i in range(width):
                waves = real_fft([Signed(increment(p, part * width + i)) for p in range(blocks)])
                at = slice(i * ROWS, (i + 1) * ROWS)
                for k, (re, im) in enumerate(waves):
                    c, s = twist_ref[0, k], twist_ref[1, k]
                    if k == 0:
                        turned = re, Signed(jnp.zeros_like(re.value))
                    elif im is None:
                        turned = re * c, -(re * s)
                    else:
                        turned = re * c + im * s, im * c - re * s
                    wave_ref[part, k, at, :LANES] = turned[0].plain()
                    wave_ref[part, k, at, LANES:] = turned[1].plain()

        def product(values, table_ref):
            high, low = split(values)
            dot = lambda a, b: jnp.dot(a, b, preferred_element_type=jnp.float32)
            return dot(low, table_ref[0]) + dot(high, table_ref[0]) + dot(high, table_ref[1])

        wave = lax.broadcasted_iota(jnp.int32, (top + 1, 1, ROWS, LANES), 0)
        wave = wave + blocks * lax.broadcasted_iota(jnp.int32, (top + 1, 1, ROWS, LANES), 3)
        kept = jnp.minimum(wave, nlon - wave) <= limit
        kept = jnp.concatenate([kept, kept], axis=-1)

        def middle(part):
            count = (top + 1) * width * ROWS
            spectrum = product(wave_ref[part].reshape(count, 2 * LANES), forward_ref)
            spectrum = spectrum.reshape(top + 1, width, ROWS, 2 * LANES)
            spectrum = jnp.where(kept, spectrum, 0.0).reshape(count, 2 * LANES)
            smooth = product(spectrum, inverse_ref)
            wave_ref[part] = smooth.reshape(top + 1, width * ROWS, 2 * LANES)

        def rebuild(part):
            for i in range(width):
                g = part * width + i
                at = slice(i * ROWS, (i + 1) * ROWS)
                waves = []
                for k in range(top + 1):
                    re, im = (
                        Signed(wave_ref[part, k, at, j : j + LANES]) for j in (0, LANES)
                    )
                    c, s = twist_ref[0, k], twist_ref[1, k]
                    if k == 0:
                        waves.append((re, None))
                    elif k == top:
                        waves.append((re * c - im * s, None))
                    else:
                        waves.append((re * c - im * s, im * c + re * s))
                for p, smooth in enumerate(real_ifft(waves)):
                    smooth = smooth.plain()
                    if not whole:
                        smooth = jnp.where(rows.polar, smooth, increment(p, g))
                    out_ref[tile(p, g), :] = x_ref[tile(p, g), :] + smooth

        parts = 8 // width
        for i in range(parts + 2):
            if i < parts:
                analyse(i)
            if 1 <= i <= parts:
                middle(i - 1)
            if i >= 2:
                rebuild(i - 2)


def on_device(state, damping, cutoff):
    fields, levels, nrow, ncol = state.shape
    bands, blocks = lax.axis_size("lat"), lax.axis_size("lon")
    chips = blocks // 2
    vmem, hbm = pl.BlockSpec(memory_space=pltpu.VMEM), pl.BlockSpec(memory_space=pltpu.HBM)
    limits = pltpu.CompilerParams(vmem_limit_bytes=40 * 2**20)

    def call(kernel, name, out, ins, outs, cost, scratch=()):
        return pl.pallas_call(
            kernel,
            out_shape=out,
            in_specs=ins,
            out_specs=outs,
            scratch_shapes=scratch,
            compiler_params=limits,
            cost_estimate=pl.CostEstimate(flops=cost, bytes_accessed=2**22, transcendentals=0),
            name=name,
        )

    def array(*shape):
        return jax.ShapeDtypeStruct(shape, jnp.float32)

    sems = [pltpu.SemaphoreType.DMA((fields, 2))]
    parts = call(
        spread_kernel, "spread", array(chips, 2, fields, 2, ROWS, ncol), [hbm], vmem, 0, sems
    )(state.reshape(fields, chips, 2, 2, ROWS, ncol))
    circles = lax.all_to_all(
        parts.reshape(blocks, -1, ncol), "lon", split_axis=0, concat_axis=0, tiled=True
    )

    twist, forward, inverse = fourier_tables(blocks)

    plane = array(8, blocks, ncol)
    z_mine = call(
        lambda *refs: pack_kernel(bands, *refs), "pack", plane, [vmem], vmem, 0
    )(circles)

    swaps = []
    for z in range(bands - 1):
        for m in range(chips):
            a, b = z * blocks + 2 * m + 1, (z + 1) * blocks + 2 * m
            swaps += [(a, b), (b, a)]
    z_other = lax.ppermute(z_mine, ("lat", "lon"), swaps)
    increments, params, c_mine, own = call(
        lambda *refs: stencil_kernel(bands, blocks, *refs),
        "stencil",
        (array(blocks * 8 * ROWS, ncol), array(3, ROWS, ncol), plane, array(4, blocks, ncol)),
        [vmem] * 3,
        (vmem,) * 4,
        2**28,
        [pltpu.VMEM((blocks, 2, ROWS, ncol), jnp.float32)],
    )(circles, damping, cutoff)
    pairs = [[2 * m, 2 * m + 1] for m in range(chips)]
    c_both = lax.all_gather(c_mine, "lon", axis_index_groups=pairs)
    moved = call(
        lambda *refs: filter_kernel(bands, blocks, *refs),
        "filter",
        array(blocks * 8 * ROWS, ncol),
        [vmem] * 9,
        vmem,
        2**31,
        [
            pltpu.VMEM((2, 10, blocks, ncol), jnp.float32),
            pltpu.VMEM((4, blocks // 2 + 1, 2 * ROWS, 2 * ncol), jnp.float32),
        ],
    )(circles.reshape(-1, ncol), increments, z_other, c_both, own, params, twist, forward, inverse)

    home = lax.all_to_all(
        moved.reshape(blocks, -1, ncol), "lon", split_axis=0, concat_axis=0, tiled=True
    )
    out = call(
        collect_kernel, "collect", array(fields, chips, 2, 2, ROWS, ncol), [vmem], hbm, 0, sems
    )(home.reshape(chips, 2, fields, 2, ROWS, ncol))
    return out.reshape(state.shape)


def solution(mesh):
    in_specs = (P(None, None, "lat", "lon"), P(), P())
    out_specs = P(None, None, "lat", "lon")
    return jax.shard_map(
        on_device, mesh=mesh, in_specs=in_specs, out_specs=out_specs, check_vma=False
    )
```

```python
import math

import jax
import jax.numpy as jnp
import numpy as np
from jax import lax
from jax.experimental import pallas as pl
from jax.experimental.pallas import tpu as pltpu
from jax.sharding import PartitionSpec as P

COURANT = 0.05
ROWS = 8
LANES = 128


def sine(angle):
    square = angle * angle
    total = jnp.zeros_like(angle)
    for n in (13, 11, 9, 7, 5, 3, 1):
        total = total * square + (-1.0) ** (n // 2) / math.factorial(n)
    return total * angle


class Rows:
    def __init__(self, bands):
        self.core = lax.axis_index("lon") % 2
        self.first = (lax.axis_index("lat") * 2 + self.core) * ROWS
        self.nlat = nlat = bands * 2 * ROWS
        row = lax.broadcasted_iota(jnp.int32, (ROWS, LANES), 0)
        near = self.first + row
        at = self.cosine(near)
        self.half = 0.5 / at
        self.up, self.down = self.cosine(near + 1) * self.half, self.cosine(near - 1) * self.half
        middle = near.astype(jnp.float32) + (0.5 - 0.5 * nlat)
        self.coriolis = 2.0 * sine(middle * (math.pi / nlat))
        self.square = at * at
        self.polar = (near < nlat // 4) | (near >= nlat - nlat // 4)
        ends = self.first + jnp.where(row < 3, row - 2, row + ROWS - 4)
        self.ends = self.cosine(ends)

    def cosine(self, row):
        index = row.astype(jnp.float32) + 0.5
        return sine(jnp.minimum(index, self.nlat - index) * (math.pi / self.nlat))

    def beside(self, side):
        below, at, above = (self.ends[side * 3 + i : side * 3 + i + 1] for i in range(3))
        row = self.first + (ROWS if side else -1)
        inside = ((row >= 0) & (row < self.nlat)).astype(jnp.float32)
        half = 0.5 / at * inside
        return (-below if side else above) * half, inside


def split(values):
    high = values.astype(jnp.bfloat16)
    low = (values - high.astype(jnp.float32)).astype(jnp.bfloat16)
    return high, low


def fourier_tables(blocks):
    nlon = blocks * LANES
    at = np.arange(LANES)
    phase = 2.0 * np.pi * ((at[:, None] * at[None, :]) % LANES) / LANES
    cos, sin = np.cos(phase), np.sin(phase)
    forward = np.block([[cos, -sin], [sin, cos]])
    inverse = np.block([[cos, sin], [-sin, cos]]) / nlon
    angle = 2.0 * np.pi * np.arange(blocks // 2 + 1)[:, None] * at[None, :] / nlon
    twice = np.where(np.arange(blocks // 2 + 1) % (blocks // 2) == 0, 1.0, math.sqrt(2.0))[:, None]
    twist = np.stack([twice * np.cos(angle), twice * np.sin(angle)]).astype(np.float32)
    twist = np.broadcast_to(twist[:, :, None, :], (2, blocks // 2 + 1, ROWS, LANES))

    def halves(matrix):
        high = matrix.astype(np.float32).astype(jnp.bfloat16)
        low = (matrix - high.astype(np.float64)).astype(np.float32).astype(jnp.bfloat16)
        return np.stack([high, low])

    return np.ascontiguousarray(twist), halves(forward), halves(inverse)


class Signed:
    def __init__(self, value, minus=False):
        self.value, self.minus = value, minus

    def __neg__(self):
        return Signed(self.value, not self.minus)

    def __add__(self, other):
        if self.minus == other.minus:
            return Signed(self.value + other.value, self.minus)
        first, second = (other, self) if self.minus else (self, other)
        return Signed(first.value - second.value)

    def __sub__(self, other):
        return self + -other

    def __mul__(self, factor):
        return Signed(self.value * factor, self.minus)

    def plain(self):
        return -self.value if self.minus else self.value


def turn(re, im, k, n):
    if 8 * k == n:
        c = math.sqrt(0.5)
        return (re + im) * c, (im - re) * c
    angle = 2.0 * math.pi * k / n
    c, s = math.cos(angle), math.sin(angle)
    return re * c + im * s, im * c - re * s


def real_fft(x):
    n = len(x)
    if n == 2:
        return [(x[0] + x[1], None), (x[0] - x[1], None)]
    even, odd = real_fft(x[0::2]), real_fft(x[1::2])
    half, quarter = n // 2, n // 4
    out = [None] * (half + 1)
    out[0] = (even[0][0] + odd[0][0], None)
    out[half] = (even[0][0] - odd[0][0], None)
    out[quarter] = (even[quarter][0], -odd[quarter][0])
    for k in range(1, quarter):
        re, im = turn(*odd[k], k, n)
        out[k] = (even[k][0] + re, even[k][1] + im)
        out[half - k] = (even[k][0] - re, im - even[k][1])
    return out


def real_ifft(w):
    half = len(w) - 1
    n, quarter = 2 * half, half // 2
    if n == 2:
        return [w[0][0] + w[1][0], w[0][0] - w[1][0]]
    even, odd = [None] * (quarter + 1), [None] * (quarter + 1)
    even[0] = (w[0][0] + w[half][0], None)
    odd[0] = (w[0][0] - w[half][0], None)
    even[quarter] = (w[quarter][0], None)
    odd[quarter] = (-w[quarter][1], None)
    for k in range(1, quarter):
        a, b = w[k], w[half - k]
        even[k] = (a[0] + b[0], a[1] - b[1])
        im, re = turn(a[1] + b[1], a[0] - b[0], k, n)
        odd[k] = (re, im)
    x = [None] * n
    x[0::2], x[1::2] = real_ifft(even), real_ifft(odd)
    return x


def rank(lon, blocks):
    return blocks - 1 - lon


def spread_kernel(x_ref, out_ref):
    fields, chips, levels, cores = x_ref.shape[:4]
    for chip in range(chips):
        for core in range(cores):
            for field in range(fields):
                for level in range(levels):
                    out_ref[chip, core, field, level] = x_ref[field, chips - 1 - chip, level, core]


def collect_kernel(x_ref, out_ref, sems):
    copies = []
    for field in range(4):
        for core in range(2):
            copies.append(
                pltpu.make_async_copy(
                    x_ref.at[:, 1 - core, field], out_ref.at[field, :, :, core], sems.at[field, core]
                )
            )
    for copy in copies:
        copy.start()
    for copy in copies:
        copy.wait()


def shifted_diff(here):
    blocks = here.shape[0]
    lane = lax.broadcasted_iota(jnp.int32, here.shape, 1)
    after = jnp.where(lane == 0, pltpu.roll(here, blocks - 1, axis=0), here)
    before = jnp.where(lane == LANES - 1, pltpu.roll(here, 1, axis=0), here)
    return pltpu.roll(after, LANES - 1, axis=1) - pltpu.roll(before, 1, axis=1)


def pack(rows, end, x_ref, out_ref):
    edge, inner = end * (ROWS - 1), 1 + end * (ROWS - 3)
    last = end == 1
    half = jnp.where(last, rows.half[ROWS - 1 :], rows.half[:1])
    weight = jnp.where(last, -rows.down[ROWS - 1 :], rows.up[:1])
    for level in range(2):

        def plane(field, row):
            return x_ref[:, (field * 2 + level) * ROWS + row, :]

        for k, field in enumerate((0, 2, 3)):
            out_ref[k * 2 + level] = plane(field, edge)
        out_ref[6 + level] = shifted_diff(plane(1, edge)) * half + weight * plane(2, inner)


def pack_kernel(bands, x_ref, z_ref):
    rows = Rows(bands)
    pack(rows, rows.core, x_ref, z_ref)


def parameters(rows, damp_ref, cutoff_ref, param_ref):
    blocks = lax.axis_size("lon")
    level = rank(lax.axis_index("lon"), blocks) // 2 * 2
    damping = damp_ref[...].reshape(1, -1)
    at = lax.broadcasted_iota(jnp.int32, damping.shape, 1)
    for i in range(2):
        one = jnp.sum(jnp.where(at == level + i, damping, 0.0), axis=1, keepdims=True)
        param_ref[i] = jnp.broadcast_to(one, (ROWS, LANES))
    cutoff = cutoff_ref[...].astype(jnp.float32).reshape(1, -1)
    cutoff = jnp.broadcast_to(cutoff, (ROWS, cutoff.shape[1]))
    at = lax.broadcasted_iota(jnp.int32, cutoff.shape, 1)
    row = lax.broadcasted_iota(jnp.int32, cutoff.shape, 0)
    limit = jnp.sum(jnp.where(at == rows.first + row, cutoff, 0.0), axis=1, keepdims=True)
    param_ref[2] = jnp.broadcast_to(limit, (ROWS, LANES))


def tile(p, g):
    start = (p * 8 + g) * ROWS
    return pl.ds(start if isinstance(start, int) else pl.multiple_of(start, ROWS), ROWS)


def stencil_kernel(
    bands, blocks, x_ref, damp_ref, cutoff_ref, inc_ref, param_ref, c_ref, own_ref, mix_ref
):
    rows = Rows(bands)
    parameters(rows, damp_ref, cutoff_ref, param_ref)
    pack(rows, 1 - rows.core, x_ref, c_ref)
    for side in range(2):
        for level in range(2):
            own_ref[side * 2 + level] = x_ref[:, (4 + level) * ROWS + side * (ROWS - 1), :]
    row = lax.broadcasted_iota(jnp.int32, (ROWS, LANES), 0)
    up = jnp.where(row == ROWS - 1, 0.0, rows.up)
    down = jnp.where(row == 0, 0.0, rows.down)
    half_up = jnp.where(row == ROWS - 1, 0.0, 0.5)
    half_down = jnp.where(row == 0, 0.0, 0.5)
    damping = [rows.square * param_ref[i] for i in range(2)]
    lane = lax.broadcasted_iota(jnp.int32, (ROWS, LANES), 1)
    first_lane, last_lane = lane == 0, lane == LANES - 1

    def zonal_diff(before, here, after):
        east = pltpu.roll(jnp.where(first_lane, after, here), LANES - 1, axis=1)
        west = pltpu.roll(jnp.where(last_lane, before, here), 1, axis=1)
        return (east - west) * rows.half

    def north(here):
        return pltpu.roll(here, ROWS - 1, axis=0)

    def south(here):
        return pltpu.roll(here, 1, axis=0)

    def x(p, g):
        return x_ref[p, pl.ds(g * ROWS, ROWS), :]

    def around(p):
        return lax.rem(p + blocks - 1, blocks), lax.rem(p + 1, blocks)

    damping_north = [south(v) for v in damping]
    damping_south = [north(v) for v in damping]

    def first_pass(p, carry):
        before, after = around(p)
        for level in range(2):
            h, u, v = level, 2 + level, 4 + level
            thick, zonal = COURANT * x(p, h), x(p, u)
            div = zonal_diff(x(before, u), zonal, x(after, u))
            div = div + up * north(x(p, v)) - down * south(x(p, v))
            mix_ref[p, level] = damping[level] * div - thick
            rise = half_up * north(damping_north[level] * div - thick)
            rise = rise - half_down * south(damping_south[level] * div - thick)
            inc_ref[tile(p, v), :] = rise - COURANT * (rows.coriolis * zonal)
        return carry

    lax.fori_loop(0, blocks, first_pass, 0, unroll=blocks)

    def second_pass(p, carry):
        before, after = around(p)
        for level in range(2):
            h, u, v, t = level, 2 + level, 4 + level, 6 + level
            zonal, merid, potential = x(p, u), x(p, v), x(p, t)
            carried = 1.0 + x(p, h)
            flux_b, flux_a = (1.0 + x(before, h)) * x(before, u), (1.0 + x(after, h)) * x(after, u)
            flow = carried * merid
            inc_ref[tile(p, h), :] = -COURANT * (
                zonal_diff(flux_b, carried * zonal, flux_a) + up * north(flow) - down * south(flow)
            )
            inc_ref[tile(p, u), :] = COURANT * (rows.coriolis * merid) + zonal_diff(
                mix_ref[before, level], mix_ref[p, level], mix_ref[after, level]
            )
            rise = half_up * north(potential) - half_down * south(potential)
            inc_ref[tile(p, t), :] = -COURANT * (
                zonal * zonal_diff(x(before, t), potential, x(after, t)) + merid * rise
            )
        return carry

    lax.fori_loop(0, blocks, second_pass, 0, unroll=blocks)


def filter_kernel(
    bands,
    blocks,
    x_ref,
    inc_ref,
    z_ref,
    c_ref,
    own_ref,
    param_ref,
    twist_ref,
    forward_ref,
    inverse_ref,
    out_ref,
    more_ref,
    wave_ref,
):
    rows = Rows(bands)
    damping = [rows.square * param_ref[i] for i in range(2)]
    for side in range(2):
        edge, inner = side * (ROWS - 1), 1 + side * (ROWS - 3)
        across, inside = rows.beside(side)
        weight = rows.up[edge : edge + 1] if side else -rows.down[edge : edge + 1]
        step = 0.5 if side else -0.5
        for level in range(2):
            damp = damping[level]
            damp_edge, damp_inner = damp[edge : edge + 1], damp[inner : inner + 1]

            def beyond(k):
                other = c_ref[1 - rows.core, k * 2 + level]
                return jnp.where(rows.core == side, z_ref[k * 2 + level], other) * inside

            thick, near, potential, div = (beyond(k) for k in range(4))
            own = own_ref[side * 2 + level]
            div = div + across * own
            extra = weight * near
            more_ref[side, level] = -COURANT * weight * ((1.0 + thick) * near)
            more_ref[side, 2 + level] = damp_edge * rows.half[edge : edge + 1] * shifted_diff(extra)
            more_ref[side, 4 + level] = step * (damp_edge * div - COURANT * thick)
            more_ref[side, 6 + level] = -COURANT * step * (own * potential)
            more_ref[side, 8 + level] = step * damp_inner * extra

    row = lax.broadcasted_iota(jnp.int32, (ROWS, LANES), 0)

    def increment(p, g):
        def more(side, k):
            return more_ref[side, k, p : p + 1, :]

        total = jnp.where(row == 0, more(0, g), jnp.where(row == ROWS - 1, more(1, g), 0.0))
        if g // 2 == 2:
            total = jnp.where(row == 1, more(0, g + 4), total)
            total = jnp.where(row == ROWS - 2, more(1, g + 4), total)
        return inc_ref[tile(p, g), :] + total

    limit = param_ref[2].astype(jnp.int32)
    any_polar = (rows.first < rows.nlat // 4) | (rows.first + ROWS > rows.nlat - rows.nlat // 4)
    whole = rows.nlat // 4 % ROWS == 0
    top = blocks // 2
    nlon = blocks * LANES

    @pl.when(jnp.logical_not(any_polar))
    def _():
        for g in range(8):
            for p in range(blocks):
                out_ref[tile(rank(p, blocks), g), :] = x_ref[tile(p, g), :] + increment(p, g)

    @pl.when(any_polar)
    def _():
        width = 2

        def analyse(part):
            for i in range(width):
                waves = real_fft([Signed(increment(p, part * width + i)) for p in range(blocks)])
                at = slice(i * ROWS, (i + 1) * ROWS)
                for k, (re, im) in enumerate(waves):
                    c, s = twist_ref[0, k], twist_ref[1, k]
                    if k == 0:
                        turned = re, Signed(jnp.zeros_like(re.value))
                    elif im is None:
                        turned = re * c, -(re * s)
                    else:
                        turned = re * c + im * s, im * c - re * s
                    wave_ref[part, k, at, :LANES] = turned[0].plain()
                    wave_ref[part, k, at, LANES:] = turned[1].plain()

        def product(values, table_ref):
            high, low = split(values)
            dot = lambda a, b: jnp.dot(a, b, preferred_element_type=jnp.float32)
            return dot(low, table_ref[0]) + dot(high, table_ref[0]) + dot(high, table_ref[1])

        wave = lax.broadcasted_iota(jnp.int32, (top + 1, 1, ROWS, LANES), 0)
        wave = wave + blocks * lax.broadcasted_iota(jnp.int32, (top + 1, 1, ROWS, LANES), 3)
        kept = jnp.minimum(wave, nlon - wave) <= limit
        kept = jnp.concatenate([kept, kept], axis=-1)

        def middle(part):
            count = (top + 1) * width * ROWS
            spectrum = product(wave_ref[part].reshape(count, 2 * LANES), forward_ref)
            spectrum = spectrum.reshape(top + 1, width, ROWS, 2 * LANES)
            spectrum = jnp.where(kept, spectrum, 0.0).reshape(count, 2 * LANES)
            smooth = product(spectrum, inverse_ref)
            wave_ref[part] = smooth.reshape(top + 1, width * ROWS, 2 * LANES)

        def rebuild(part):
            for i in range(width):
                g = part * width + i
                at = slice(i * ROWS, (i + 1) * ROWS)
                waves = []
                for k in range(top + 1):
                    re, im = (
                        Signed(wave_ref[part, k, at, j : j + LANES]) for j in (0, LANES)
                    )
                    c, s = twist_ref[0, k], twist_ref[1, k]
                    if k == 0:
                        waves.append((re, None))
                    elif k == top:
                        waves.append((re * c - im * s, None))
                    else:
                        waves.append((re * c - im * s, im * c + re * s))
                for p, smooth in enumerate(real_ifft(waves)):
                    smooth = smooth.plain()
                    if not whole:
                        smooth = jnp.where(rows.polar, smooth, increment(p, g))
                    out_ref[tile(rank(p, blocks), g), :] = x_ref[tile(p, g), :] + smooth

        parts = 8 // width
        for i in range(parts + 2):
            if i < parts:
                analyse(i)
            if 1 <= i <= parts:
                middle(i - 1)
            if i >= 2:
                rebuild(i - 2)


def on_device(state, damping, cutoff):
    fields, levels, nrow, ncol = state.shape
    bands, blocks = lax.axis_size("lat"), lax.axis_size("lon")
    chips = blocks // 2
    vmem, hbm = pl.BlockSpec(memory_space=pltpu.VMEM), pl.BlockSpec(memory_space=pltpu.HBM)
    limits = pltpu.CompilerParams(vmem_limit_bytes=40 * 2**20)

    def call(kernel, name, out, ins, outs, cost, scratch=()):
        return pl.pallas_call(
            kernel,
            out_shape=out,
            in_specs=ins,
            out_specs=outs,
            scratch_shapes=scratch,
            compiler_params=limits,
            cost_estimate=pl.CostEstimate(flops=cost, bytes_accessed=2**22, transcendentals=0),
            name=name,
        )

    def array(*shape):
        return jax.ShapeDtypeStruct(shape, jnp.float32)

    sems = [pltpu.SemaphoreType.DMA((fields, 2))]
    parts = call(
        spread_kernel, "spread", array(chips, 2, fields, 2, ROWS, ncol), [vmem], vmem, 0
    )(state.reshape(fields, chips, 2, 2, ROWS, ncol))
    circles = lax.all_to_all(
        parts.reshape(blocks, -1, ncol), "lon", split_axis=0, concat_axis=0, tiled=True
    )

    twist, forward, inverse = fourier_tables(blocks)

    plane = array(8, blocks, ncol)
    z_mine = call(
        lambda *refs: pack_kernel(bands, *refs), "pack", plane, [vmem], vmem, 0
    )(circles)

    swaps = []
    for z in range(bands - 1):
        for m in range(chips):
            a, b = z * blocks + 2 * m + 1, (z + 1) * blocks + 2 * m
            swaps += [(a, b), (b, a)]
    z_other = lax.ppermute(z_mine, ("lat", "lon"), swaps)
    increments, params, c_mine, own = call(
        lambda *refs: stencil_kernel(bands, blocks, *refs),
        "stencil",
        (array(blocks * 8 * ROWS, ncol), array(3, ROWS, ncol), plane, array(4, blocks, ncol)),
        [vmem] * 3,
        (vmem,) * 4,
        2**28,
        [pltpu.VMEM((blocks, 2, ROWS, ncol), jnp.float32)],
    )(circles, damping, cutoff)
    pairs = [[2 * m, 2 * m + 1] for m in range(chips)]
    c_both = lax.all_gather(c_mine, "lon", axis_index_groups=pairs)
    moved = call(
        lambda *refs: filter_kernel(bands, blocks, *refs),
        "filter",
        array(blocks * 8 * ROWS, ncol),
        [vmem] * 9,
        vmem,
        2**31,
        [
            pltpu.VMEM((2, 10, blocks, ncol), jnp.float32),
            pltpu.VMEM((4, blocks // 2 + 1, 2 * ROWS, 2 * ncol), jnp.float32),
        ],
    )(circles.reshape(-1, ncol), increments, z_other, c_both, own, params, twist, forward, inverse)

    home = lax.all_to_all(
        moved.reshape(blocks, -1, ncol),
        "lon",
        split_axis=0,
        concat_axis=0,
        axis_index_groups=[[rank(lon, blocks) for lon in range(blocks)]],
        tiled=True,
    )
    out = call(
        collect_kernel, "collect", array(fields, chips, 2, 2, ROWS, ncol), [vmem], hbm, 0, sems
    )(home.reshape(chips, 2, fields, 2, ROWS, ncol))
    return out.reshape(state.shape)


def solution(mesh):
    in_specs = (P(None, None, "lat", "lon"), P(), P())
    out_specs = P(None, None, "lat", "lon")
    return jax.shard_map(
        on_device, mesh=mesh, in_specs=in_specs, out_specs=out_specs, check_vma=False
    )
```

```python
import math

import jax
import jax.numpy as jnp
import numpy as np
from jax import lax
from jax.experimental import pallas as pl
from jax.experimental.pallas import tpu as pltpu
from jax.sharding import PartitionSpec as P

COURANT = 0.05
ROWS = 8
LANES = 128


def sine(angle):
    square = angle * angle
    total = jnp.zeros_like(angle)
    for n in (13, 11, 9, 7, 5, 3, 1):
        total = total * square + (-1.0) ** (n // 2) / math.factorial(n)
    return total * angle


class Rows:
    def __init__(self, bands):
        self.core = lax.axis_index("lon") % 2
        self.first = (lax.axis_index("lat") * 2 + self.core) * ROWS
        self.nlat = nlat = bands * 2 * ROWS
        row = lax.broadcasted_iota(jnp.int32, (ROWS, LANES), 0)
        near = self.first + row
        at = self.cosine(near)
        self.half = 0.5 / at
        self.up, self.down = self.cosine(near + 1) * self.half, self.cosine(near - 1) * self.half
        middle = near.astype(jnp.float32) + (0.5 - 0.5 * nlat)
        self.coriolis = 2.0 * sine(middle * (math.pi / nlat))
        self.square = at * at
        self.polar = (near < nlat // 4) | (near >= nlat - nlat // 4)
        ends = self.first + jnp.where(row < 3, row - 2, row + ROWS - 4)
        self.ends = self.cosine(ends)

    def cosine(self, row):
        index = row.astype(jnp.float32) + 0.5
        return sine(jnp.minimum(index, self.nlat - index) * (math.pi / self.nlat))

    def beside(self, side):
        below, at, above = (self.ends[side * 3 + i : side * 3 + i + 1] for i in range(3))
        row = self.first + (ROWS if side else -1)
        inside = ((row >= 0) & (row < self.nlat)).astype(jnp.float32)
        half = 0.5 / at * inside
        return (-below if side else above) * half, inside


def split(values):
    high = values.astype(jnp.bfloat16)
    low = (values - high.astype(jnp.float32)).astype(jnp.bfloat16)
    return high, low


def fourier_tables(blocks):
    nlon = blocks * LANES
    at = np.arange(LANES)
    phase = 2.0 * np.pi * ((at[:, None] * at[None, :]) % LANES) / LANES
    cos, sin = np.cos(phase), np.sin(phase)
    forward = np.block([[cos, -sin], [sin, cos]])
    inverse = np.block([[cos, sin], [-sin, cos]]) / nlon
    angle = 2.0 * np.pi * np.arange(blocks // 2 + 1)[:, None] * at[None, :] / nlon
    twice = np.where(np.arange(blocks // 2 + 1) % (blocks // 2) == 0, 1.0, math.sqrt(2.0))[:, None]
    twist = np.stack([twice * np.cos(angle), twice * np.sin(angle)]).astype(np.float32)
    twist = np.broadcast_to(twist[:, :, None, :], (2, blocks // 2 + 1, ROWS, LANES))

    def halves(matrix):
        high = matrix.astype(np.float32).astype(jnp.bfloat16)
        low = (matrix - high.astype(np.float64)).astype(np.float32).astype(jnp.bfloat16)
        return np.stack([high, low])

    return np.ascontiguousarray(twist), halves(forward), halves(inverse)


class Signed:
    def __init__(self, value, minus=False):
        self.value, self.minus = value, minus

    def __neg__(self):
        return Signed(self.value, not self.minus)

    def __add__(self, other):
        if self.minus == other.minus:
            return Signed(self.value + other.value, self.minus)
        first, second = (other, self) if self.minus else (self, other)
        return Signed(first.value - second.value)

    def __sub__(self, other):
        return self + -other

    def __mul__(self, factor):
        return Signed(self.value * factor, self.minus)

    def plain(self):
        return -self.value if self.minus else self.value


def turn(re, im, k, n):
    if 8 * k == n:
        c = math.sqrt(0.5)
        return (re + im) * c, (im - re) * c
    angle = 2.0 * math.pi * k / n
    c, s = math.cos(angle), math.sin(angle)
    return re * c + im * s, im * c - re * s


def real_fft(x):
    n = len(x)
    if n == 2:
        return [(x[0] + x[1], None), (x[0] - x[1], None)]
    even, odd = real_fft(x[0::2]), real_fft(x[1::2])
    half, quarter = n // 2, n // 4
    out = [None] * (half + 1)
    out[0] = (even[0][0] + odd[0][0], None)
    out[half] = (even[0][0] - odd[0][0], None)
    out[quarter] = (even[quarter][0], -odd[quarter][0])
    for k in range(1, quarter):
        re, im = turn(*odd[k], k, n)
        out[k] = (even[k][0] + re, even[k][1] + im)
        out[half - k] = (even[k][0] - re, im - even[k][1])
    return out


def real_ifft(w):
    half = len(w) - 1
    n, quarter = 2 * half, half // 2
    if n == 2:
        return [w[0][0] + w[1][0], w[0][0] - w[1][0]]
    even, odd = [None] * (quarter + 1), [None] * (quarter + 1)
    even[0] = (w[0][0] + w[half][0], None)
    odd[0] = (w[0][0] - w[half][0], None)
    even[quarter] = (w[quarter][0], None)
    odd[quarter] = (-w[quarter][1], None)
    for k in range(1, quarter):
        a, b = w[k], w[half - k]
        even[k] = (a[0] + b[0], a[1] - b[1])
        im, re = turn(a[1] + b[1], a[0] - b[0], k, n)
        odd[k] = (re, im)
    x = [None] * n
    x[0::2], x[1::2] = real_ifft(even), real_ifft(odd)
    return x


def way_back(blocks):
    first = blocks // 2 + blocks // 8 + 1
    return [first] + [lon for lon in range(blocks - 1, -1, -1) if lon != first]


def spread_kernel(x_ref, out_ref):
    fields, chips, levels, cores = x_ref.shape[:4]
    for chip in range(chips):
        for core in range(cores):
            for field in range(fields):
                for level in range(levels):
                    out_ref[chip, core, field, level] = x_ref[field, chip, level, core]


def collect_kernel(x_ref, out_ref, held_ref, sems):
    fields, chips, levels, cores = out_ref.shape[:4]
    order = way_back(chips * cores)
    copies = []
    for field in range(fields):
        for half in range(2):
            part = pl.ds(half * chips // 2, chips // 2)
            for chip in range(half * chips // 2, (half + 1) * chips // 2):
                for core in range(cores):
                    for level in range(levels):
                        here = x_ref[order.index(chip * cores + core), field, level]
                        held_ref[field, chip, level, core] = here
            copies.append(
                pltpu.make_async_copy(
                    held_ref.at[field, part], out_ref.at[field, part], sems.at[field, half]
                )
            )
            copies[-1].start()
    for copy in copies:
        copy.wait()


def shifted_diff(here):
    blocks = here.shape[0]
    lane = lax.broadcasted_iota(jnp.int32, here.shape, 1)
    after = jnp.where(lane == 0, pltpu.roll(here, blocks - 1, axis=0), here)
    before = jnp.where(lane == LANES - 1, pltpu.roll(here, 1, axis=0), here)
    return pltpu.roll(after, LANES - 1, axis=1) - pltpu.roll(before, 1, axis=1)


def pack(rows, end, x_ref, out_ref):
    edge, inner = end * (ROWS - 1), 1 + end * (ROWS - 3)
    last = end == 1
    half = jnp.where(last, rows.half[ROWS - 1 :], rows.half[:1])
    weight = jnp.where(last, -rows.down[ROWS - 1 :], rows.up[:1])
    for level in range(2):

        def plane(field, row):
            return x_ref[:, (field * 2 + level) * ROWS + row, :]

        for k, field in enumerate((0, 2, 3)):
            out_ref[k * 2 + level] = plane(field, edge)
        out_ref[6 + level] = shifted_diff(plane(1, edge)) * half + weight * plane(2, inner)


def pack_kernel(bands, x_ref, z_ref):
    rows = Rows(bands)
    pack(rows, rows.core, x_ref, z_ref)


def parameters(rows, damp_ref, cutoff_ref, param_ref):
    level = lax.axis_index("lon") // 2 * 2
    damping = damp_ref[...].reshape(1, -1)
    at = lax.broadcasted_iota(jnp.int32, damping.shape, 1)
    for i in range(2):
        one = jnp.sum(jnp.where(at == level + i, damping, 0.0), axis=1, keepdims=True)
        param_ref[i] = jnp.broadcast_to(one, (ROWS, LANES))
    cutoff = cutoff_ref[...].astype(jnp.float32).reshape(1, -1)
    cutoff = jnp.broadcast_to(cutoff, (ROWS, cutoff.shape[1]))
    at = lax.broadcasted_iota(jnp.int32, cutoff.shape, 1)
    row = lax.broadcasted_iota(jnp.int32, cutoff.shape, 0)
    limit = jnp.sum(jnp.where(at == rows.first + row, cutoff, 0.0), axis=1, keepdims=True)
    param_ref[2] = jnp.broadcast_to(limit, (ROWS, LANES))


def tile(p, g):
    start = (p * 8 + g) * ROWS
    return pl.ds(start if isinstance(start, int) else pl.multiple_of(start, ROWS), ROWS)


def stencil_kernel(
    bands, blocks, x_ref, damp_ref, cutoff_ref, inc_ref, param_ref, c_ref, own_ref, mix_ref
):
    rows = Rows(bands)
    parameters(rows, damp_ref, cutoff_ref, param_ref)
    pack(rows, 1 - rows.core, x_ref, c_ref)
    for side in range(2):
        for level in range(2):
            own_ref[side * 2 + level] = x_ref[:, (4 + level) * ROWS + side * (ROWS - 1), :]
    row = lax.broadcasted_iota(jnp.int32, (ROWS, LANES), 0)
    up = jnp.where(row == ROWS - 1, 0.0, rows.up)
    down = jnp.where(row == 0, 0.0, rows.down)
    half_up = jnp.where(row == ROWS - 1, 0.0, 0.5)
    half_down = jnp.where(row == 0, 0.0, 0.5)
    damping = [rows.square * param_ref[i] for i in range(2)]
    lane = lax.broadcasted_iota(jnp.int32, (ROWS, LANES), 1)
    first_lane, last_lane = lane == 0, lane == LANES - 1

    def zonal_diff(before, here, after):
        east = pltpu.roll(jnp.where(first_lane, after, here), LANES - 1, axis=1)
        west = pltpu.roll(jnp.where(last_lane, before, here), 1, axis=1)
        return (east - west) * rows.half

    def north(here):
        return pltpu.roll(here, ROWS - 1, axis=0)

    def south(here):
        return pltpu.roll(here, 1, axis=0)

    def x(p, g):
        return x_ref[p, pl.ds(g * ROWS, ROWS), :]

    def around(p):
        return lax.rem(p + blocks - 1, blocks), lax.rem(p + 1, blocks)

    damping_north = [south(v) for v in damping]
    damping_south = [north(v) for v in damping]

    def first_pass(p, carry):
        before, after = around(p)
        for level in range(2):
            h, u, v = level, 2 + level, 4 + level
            thick, zonal = COURANT * x(p, h), x(p, u)
            div = zonal_diff(x(before, u), zonal, x(after, u))
            div = div + up * north(x(p, v)) - down * south(x(p, v))
            mix_ref[p, level] = damping[level] * div - thick
            rise = half_up * north(damping_north[level] * div - thick)
            rise = rise - half_down * south(damping_south[level] * div - thick)
            inc_ref[tile(p, v), :] = rise - COURANT * (rows.coriolis * zonal)
        return carry

    lax.fori_loop(0, blocks, first_pass, 0, unroll=blocks)

    def second_pass(p, carry):
        before, after = around(p)
        for level in range(2):
            h, u, v, t = level, 2 + level, 4 + level, 6 + level
            zonal, merid, potential = x(p, u), x(p, v), x(p, t)
            carried = 1.0 + x(p, h)
            flux_b, flux_a = (1.0 + x(before, h)) * x(before, u), (1.0 + x(after, h)) * x(after, u)
            flow = carried * merid
            inc_ref[tile(p, h), :] = -COURANT * (
                zonal_diff(flux_b, carried * zonal, flux_a) + up * north(flow) - down * south(flow)
            )
            inc_ref[tile(p, u), :] = COURANT * (rows.coriolis * merid) + zonal_diff(
                mix_ref[before, level], mix_ref[p, level], mix_ref[after, level]
            )
            rise = half_up * north(potential) - half_down * south(potential)
            inc_ref[tile(p, t), :] = -COURANT * (
                zonal * zonal_diff(x(before, t), potential, x(after, t)) + merid * rise
            )
        return carry

    lax.fori_loop(0, blocks, second_pass, 0, unroll=blocks)


def filter_kernel(
    bands,
    blocks,
    x_ref,
    inc_ref,
    z_ref,
    c_ref,
    own_ref,
    param_ref,
    twist_ref,
    forward_ref,
    inverse_ref,
    out_ref,
    more_ref,
    wave_ref,
):
    rows = Rows(bands)
    damping = [rows.square * param_ref[i] for i in range(2)]
    for side in range(2):
        edge, inner = side * (ROWS - 1), 1 + side * (ROWS - 3)
        across, inside = rows.beside(side)
        weight = rows.up[edge : edge + 1] if side else -rows.down[edge : edge + 1]
        step = 0.5 if side else -0.5
        for level in range(2):
            damp = damping[level]
            damp_edge, damp_inner = damp[edge : edge + 1], damp[inner : inner + 1]

            def beyond(k):
                other = c_ref[1 - rows.core, k * 2 + level]
                return jnp.where(rows.core == side, z_ref[k * 2 + level], other) * inside

            thick, near, potential, div = (beyond(k) for k in range(4))
            own = own_ref[side * 2 + level]
            div = div + across * own
            extra = weight * near
            more_ref[side, level] = -COURANT * weight * ((1.0 + thick) * near)
            more_ref[side, 2 + level] = damp_edge * rows.half[edge : edge + 1] * shifted_diff(extra)
            more_ref[side, 4 + level] = step * (damp_edge * div - COURANT * thick)
            more_ref[side, 6 + level] = -COURANT * step * (own * potential)
            more_ref[side, 8 + level] = step * damp_inner * extra

    row = lax.broadcasted_iota(jnp.int32, (ROWS, LANES), 0)
    order = way_back(blocks)

    def increment(p, g):
        def more(side, k):
            return more_ref[side, k, p : p + 1, :]

        total = jnp.where(row == 0, more(0, g), jnp.where(row == ROWS - 1, more(1, g), 0.0))
        if g // 2 == 2:
            total = jnp.where(row == 1, more(0, g + 4), total)
            total = jnp.where(row == ROWS - 2, more(1, g + 4), total)
        return inc_ref[tile(p, g), :] + total

    limit = param_ref[2].astype(jnp.int32)
    any_polar = (rows.first < rows.nlat // 4) | (rows.first + ROWS > rows.nlat - rows.nlat // 4)
    whole = rows.nlat // 4 % ROWS == 0
    top = blocks // 2
    nlon = blocks * LANES

    @pl.when(jnp.logical_not(any_polar))
    def _():
        for g in range(8):
            for p in range(blocks):
                out_ref[tile(order.index(p), g), :] = x_ref[tile(p, g), :] + increment(p, g)

    @pl.when(any_polar)
    def _():
        width = 2

        def analyse(part):
            for i in range(width):
                waves = real_fft([Signed(increment(p, part * width + i)) for p in range(blocks)])
                at = slice(i * ROWS, (i + 1) * ROWS)
                for k, (re, im) in enumerate(waves):
                    c, s = twist_ref[0, k], twist_ref[1, k]
                    if k == 0:
                        turned = re, Signed(jnp.zeros_like(re.value))
                    elif im is None:
                        turned = re * c, -(re * s)
                    else:
                        turned = re * c + im * s, im * c - re * s
                    wave_ref[part, k, at, :LANES] = turned[0].plain()
                    wave_ref[part, k, at, LANES:] = turned[1].plain()

        def product(values, table_ref):
            high, low = split(values)
            dot = lambda a, b: jnp.dot(a, b, preferred_element_type=jnp.float32)
            return dot(low, table_ref[0]) + dot(high, table_ref[0]) + dot(high, table_ref[1])

        wave = lax.broadcasted_iota(jnp.int32, (top + 1, 1, ROWS, LANES), 0)
        wave = wave + blocks * lax.broadcasted_iota(jnp.int32, (top + 1, 1, ROWS, LANES), 3)
        kept = jnp.minimum(wave, nlon - wave) <= limit
        kept = jnp.concatenate([kept, kept], axis=-1)

        def middle(part):
            count = (top + 1) * width * ROWS
            spectrum = product(wave_ref[part].reshape(count, 2 * LANES), forward_ref)
            spectrum = spectrum.reshape(top + 1, width, ROWS, 2 * LANES)
            spectrum = jnp.where(kept, spectrum, 0.0).reshape(count, 2 * LANES)
            smooth = product(spectrum, inverse_ref)
            wave_ref[part] = smooth.reshape(top + 1, width * ROWS, 2 * LANES)

        def rebuild(part):
            for i in range(width):
                g = part * width + i
                at = slice(i * ROWS, (i + 1) * ROWS)
                waves = []
                for k in range(top + 1):
                    re, im = (
                        Signed(wave_ref[part, k, at, j : j + LANES]) for j in (0, LANES)
                    )
                    c, s = twist_ref[0, k], twist_ref[1, k]
                    if k == 0:
                        waves.append((re, None))
                    elif k == top:
                        waves.append((re * c - im * s, None))
                    else:
                        waves.append((re * c - im * s, im * c + re * s))
                for p, smooth in enumerate(real_ifft(waves)):
                    smooth = smooth.plain()
                    if not whole:
                        smooth = jnp.where(rows.polar, smooth, increment(p, g))
                    out_ref[tile(order.index(p), g), :] = x_ref[tile(p, g), :] + smooth

        parts = 8 // width
        for i in range(parts + 2):
            if i < parts:
                analyse(i)
            if 1 <= i <= parts:
                middle(i - 1)
            if i >= 2:
                rebuild(i - 2)


def on_device(state, damping, cutoff):
    fields, levels, nrow, ncol = state.shape
    bands, blocks = lax.axis_size("lat"), lax.axis_size("lon")
    chips = blocks // 2
    vmem, hbm = pl.BlockSpec(memory_space=pltpu.VMEM), pl.BlockSpec(memory_space=pltpu.HBM)
    limits = pltpu.CompilerParams(vmem_limit_bytes=40 * 2**20)

    def call(kernel, name, out, ins, outs, cost, scratch=()):
        return pl.pallas_call(
            kernel,
            out_shape=out,
            in_specs=ins,
            out_specs=outs,
            scratch_shapes=scratch,
            compiler_params=limits,
            cost_estimate=pl.CostEstimate(flops=cost, bytes_accessed=2**22, transcendentals=0),
            name=name,
        )

    def array(*shape):
        return jax.ShapeDtypeStruct(shape, jnp.float32)

    parts = call(
        spread_kernel, "spread", array(chips, 2, fields, 2, ROWS, ncol), [vmem], vmem, 0
    )(state.reshape(fields, chips, 2, 2, ROWS, ncol))
    circles = lax.all_to_all(
        parts.reshape(blocks, -1, ncol), "lon", split_axis=0, concat_axis=0, tiled=True
    )

    twist, forward, inverse = fourier_tables(blocks)

    plane = array(8, blocks, ncol)
    z_mine = call(
        lambda *refs: pack_kernel(bands, *refs), "pack", plane, [vmem], vmem, 0
    )(circles)

    swaps = []
    for z in range(bands - 1):
        for m in range(chips):
            a, b = z * blocks + 2 * m + 1, (z + 1) * blocks + 2 * m
            swaps += [(a, b), (b, a)]
    z_other = lax.ppermute(z_mine, ("lat", "lon"), swaps)
    increments, params, c_mine, own = call(
        lambda *refs: stencil_kernel(bands, blocks, *refs),
        "stencil",
        (array(blocks * 8 * ROWS, ncol), array(3, ROWS, ncol), plane, array(4, blocks, ncol)),
        [vmem] * 3,
        (vmem,) * 4,
        2**28,
        [pltpu.VMEM((blocks, 2, ROWS, ncol), jnp.float32)],
    )(circles, damping, cutoff)
    pairs = [[2 * m, 2 * m + 1] for m in range(chips)]
    c_both = lax.all_gather(c_mine, "lon", axis_index_groups=pairs)
    moved = call(
        lambda *refs: filter_kernel(bands, blocks, *refs),
        "filter",
        array(blocks * 8 * ROWS, ncol),
        [vmem] * 9,
        vmem,
        2**31,
        [
            pltpu.VMEM((2, 10, blocks, ncol), jnp.float32),
            pltpu.VMEM((4, blocks // 2 + 1, 2 * ROWS, 2 * ncol), jnp.float32),
        ],
    )(circles.reshape(-1, ncol), increments, z_other, c_both, own, params, twist, forward, inverse)

    home = lax.all_to_all(
        moved.reshape(blocks, -1, ncol),
        "lon",
        split_axis=0,
        concat_axis=0,
        axis_index_groups=[way_back(blocks)],
        tiled=True,
    )
    whole = (fields, chips, 2, 2, ROWS, ncol)
    out = call(
        collect_kernel,
        "collect",
        array(*whole),
        [vmem],
        hbm,
        0,
        [pltpu.VMEM(whole, jnp.float32), pltpu.SemaphoreType.DMA((fields, 2))],
    )(home.reshape(blocks, fields, 2, ROWS, ncol))
    return out.reshape(state.shape)


def solution(mesh):
    in_specs = (P(None, None, "lat", "lon"), P(), P())
    out_specs = P(None, None, "lat", "lon")
    return jax.shard_map(
        on_device, mesh=mesh, in_specs=in_specs, out_specs=out_specs, check_vma=False
    )
```

```python
import math

import jax
import jax.numpy as jnp
import numpy as np
from jax import lax
from jax.experimental import pallas as pl
from jax.experimental.pallas import tpu as pltpu
from jax.sharding import PartitionSpec as P

COURANT = 0.05
ROWS = 8
LANES = 128


def sine(angle):
    square = angle * angle
    total = jnp.zeros_like(angle)
    for n in (13, 11, 9, 7, 5, 3, 1):
        total = total * square + (-1.0) ** (n // 2) / math.factorial(n)
    return total * angle


class Rows:
    def __init__(self, bands):
        self.core = lax.axis_index("lon") % 2
        self.first = (lax.axis_index("lat") * 2 + self.core) * ROWS
        self.nlat = nlat = bands * 2 * ROWS
        row = lax.broadcasted_iota(jnp.int32, (ROWS, LANES), 0)
        near = self.first + row
        at = self.cosine(near)
        self.half = 0.5 / at
        self.up, self.down = self.cosine(near + 1) * self.half, self.cosine(near - 1) * self.half
        middle = near.astype(jnp.float32) + (0.5 - 0.5 * nlat)
        self.coriolis = 2.0 * sine(middle * (math.pi / nlat))
        self.square = at * at
        self.polar = (near < nlat // 4) | (near >= nlat - nlat // 4)
        ends = self.first + jnp.where(row < 3, row - 2, row + ROWS - 4)
        self.ends = self.cosine(ends)

    def cosine(self, row):
        index = row.astype(jnp.float32) + 0.5
        return sine(jnp.minimum(index, self.nlat - index) * (math.pi / self.nlat))

    def beside(self, side):
        below, at, above = (self.ends[side * 3 + i : side * 3 + i + 1] for i in range(3))
        row = self.first + (ROWS if side else -1)
        inside = ((row >= 0) & (row < self.nlat)).astype(jnp.float32)
        half = 0.5 / at * inside
        return (-below if side else above) * half, inside


def split(values):
    high = values.astype(jnp.bfloat16)
    low = (values - high.astype(jnp.float32)).astype(jnp.bfloat16)
    return high, low


def fourier_tables(blocks):
    nlon = blocks * LANES
    at = np.arange(LANES)
    phase = 2.0 * np.pi * ((at[:, None] * at[None, :]) % LANES) / LANES
    cos, sin = np.cos(phase), np.sin(phase)
    forward = np.block([[cos, -sin], [sin, cos]])
    inverse = np.block([[cos, sin], [-sin, cos]]) / nlon
    angle = 2.0 * np.pi * np.arange(blocks // 2 + 1)[:, None] * at[None, :] / nlon
    twice = np.where(np.arange(blocks // 2 + 1) % (blocks // 2) == 0, 1.0, math.sqrt(2.0))[:, None]
    twist = np.stack([twice * np.cos(angle), twice * np.sin(angle)]).astype(np.float32)
    twist = np.broadcast_to(twist[:, :, None, :], (2, blocks // 2 + 1, ROWS, LANES))

    def halves(matrix):
        high = matrix.astype(np.float32).astype(jnp.bfloat16)
        low = (matrix - high.astype(np.float64)).astype(np.float32).astype(jnp.bfloat16)
        return np.stack([high, low])

    return np.ascontiguousarray(twist), halves(forward), halves(inverse)


class Signed:
    def __init__(self, value, minus=False):
        self.value, self.minus = value, minus

    def __neg__(self):
        return Signed(self.value, not self.minus)

    def __add__(self, other):
        if self.minus == other.minus:
            return Signed(self.value + other.value, self.minus)
        first, second = (other, self) if self.minus else (self, other)
        return Signed(first.value - second.value)

    def __sub__(self, other):
        return self + -other

    def __mul__(self, factor):
        return Signed(self.value * factor, self.minus)

    def plain(self):
        return -self.value if self.minus else self.value


def turn(re, im, k, n):
    if 8 * k == n:
        c = math.sqrt(0.5)
        return (re + im) * c, (im - re) * c
    angle = 2.0 * math.pi * k / n
    c, s = math.cos(angle), math.sin(angle)
    return re * c + im * s, im * c - re * s


def real_fft(x):
    n = len(x)
    if n == 2:
        return [(x[0] + x[1], None), (x[0] - x[1], None)]
    even, odd = real_fft(x[0::2]), real_fft(x[1::2])
    half, quarter = n // 2, n // 4
    out = [None] * (half + 1)
    out[0] = (even[0][0] + odd[0][0], None)
    out[half] = (even[0][0] - odd[0][0], None)
    out[quarter] = (even[quarter][0], -odd[quarter][0])
    for k in range(1, quarter):
        re, im = turn(*odd[k], k, n)
        out[k] = (even[k][0] + re, even[k][1] + im)
        out[half - k] = (even[k][0] - re, im - even[k][1])
    return out


def real_ifft(w):
    half = len(w) - 1
    n, quarter = 2 * half, half // 2
    if n == 2:
        return [w[0][0] + w[1][0], w[0][0] - w[1][0]]
    even, odd = [None] * (quarter + 1), [None] * (quarter + 1)
    even[0] = (w[0][0] + w[half][0], None)
    odd[0] = (w[0][0] - w[half][0], None)
    even[quarter] = (w[quarter][0], None)
    odd[quarter] = (-w[quarter][1], None)
    for k in range(1, quarter):
        a, b = w[k], w[half - k]
        even[k] = (a[0] + b[0], a[1] - b[1])
        im, re = turn(a[1] + b[1], a[0] - b[0], k, n)
        odd[k] = (re, im)
    x = [None] * n
    x[0::2], x[1::2] = real_ifft(even), real_ifft(odd)
    return x


def way_back(blocks):
    first = blocks // 2 + blocks // 8 + 1
    return [first] + [lon for lon in range(blocks) if lon != first]


def spread_kernel(x_ref, out_ref):
    fields, chips, levels, cores = x_ref.shape[:4]
    for chip in range(chips):
        for core in range(cores):
            for field in range(fields):
                for level in range(levels):
                    out_ref[chip, core, field, level] = x_ref[field, chip, level, core]


def collect_kernel(x_ref, out_ref, held_ref, sems):
    fields, chips, levels, cores = out_ref.shape[:4]
    order = way_back(chips * cores)
    copies = []
    for field in range(fields):
        for half in range(2):
            part = pl.ds(half * chips // 2, chips // 2)
            for chip in range(half * chips // 2, (half + 1) * chips // 2):
                for core in range(cores):
                    for level in range(levels):
                        here = x_ref[order.index(chip * cores + core), field, level]
                        held_ref[field, chip, level, core] = here
            copies.append(
                pltpu.make_async_copy(
                    held_ref.at[field, part], out_ref.at[field, part], sems.at[field, half]
                )
            )
            copies[-1].start()
    for copy in copies:
        copy.wait()


def shifted_diff(here):
    blocks = here.shape[0]
    lane = lax.broadcasted_iota(jnp.int32, here.shape, 1)
    after = jnp.where(lane == 0, pltpu.roll(here, blocks - 1, axis=0), here)
    before = jnp.where(lane == LANES - 1, pltpu.roll(here, 1, axis=0), here)
    return pltpu.roll(after, LANES - 1, axis=1) - pltpu.roll(before, 1, axis=1)


def pack(rows, end, x_ref, out_ref):
    edge, inner = end * (ROWS - 1), 1 + end * (ROWS - 3)
    last = end == 1
    half = jnp.where(last, rows.half[ROWS - 1 :], rows.half[:1])
    weight = jnp.where(last, -rows.down[ROWS - 1 :], rows.up[:1])
    for level in range(2):

        def plane(field, row):
            return x_ref[:, (field * 2 + level) * ROWS + row, :]

        for k, field in enumerate((0, 2, 3)):
            out_ref[k * 2 + level] = plane(field, edge)
        out_ref[6 + level] = shifted_diff(plane(1, edge)) * half + weight * plane(2, inner)


def pack_kernel(bands, x_ref, z_ref):
    rows = Rows(bands)
    pack(rows, rows.core, x_ref, z_ref)


def parameters(rows, damp_ref, cutoff_ref, param_ref):
    level = lax.axis_index("lon") // 2 * 2
    damping = damp_ref[...].reshape(1, -1)
    at = lax.broadcasted_iota(jnp.int32, damping.shape, 1)
    for i in range(2):
        one = jnp.sum(jnp.where(at == level + i, damping, 0.0), axis=1, keepdims=True)
        param_ref[i] = jnp.broadcast_to(one, (ROWS, LANES))
    cutoff = cutoff_ref[...].astype(jnp.float32).reshape(1, -1)
    cutoff = jnp.broadcast_to(cutoff, (ROWS, cutoff.shape[1]))
    at = lax.broadcasted_iota(jnp.int32, cutoff.shape, 1)
    row = lax.broadcasted_iota(jnp.int32, cutoff.shape, 0)
    limit = jnp.sum(jnp.where(at == rows.first + row, cutoff, 0.0), axis=1, keepdims=True)
    param_ref[2] = jnp.broadcast_to(limit, (ROWS, LANES))


def tile(p, g):
    start = (p * 8 + g) * ROWS
    return pl.ds(start if isinstance(start, int) else pl.multiple_of(start, ROWS), ROWS)


def stencil_kernel(
    bands, blocks, x_ref, damp_ref, cutoff_ref, inc_ref, param_ref, c_ref, own_ref, mix_ref
):
    rows = Rows(bands)
    parameters(rows, damp_ref, cutoff_ref, param_ref)
    pack(rows, 1 - rows.core, x_ref, c_ref)
    for side in range(2):
        for level in range(2):
            own_ref[side * 2 + level] = x_ref[:, (4 + level) * ROWS + side * (ROWS - 1), :]
    row = lax.broadcasted_iota(jnp.int32, (ROWS, LANES), 0)
    up = jnp.where(row == ROWS - 1, 0.0, rows.up)
    down = jnp.where(row == 0, 0.0, rows.down)
    half_up = jnp.where(row == ROWS - 1, 0.0, 0.5)
    half_down = jnp.where(row == 0, 0.0, 0.5)
    damping = [rows.square * param_ref[i] for i in range(2)]
    lane = lax.broadcasted_iota(jnp.int32, (ROWS, LANES), 1)
    first_lane, last_lane = lane == 0, lane == LANES - 1

    def zonal_diff(before, here, after):
        east = pltpu.roll(jnp.where(first_lane, after, here), LANES - 1, axis=1)
        west = pltpu.roll(jnp.where(last_lane, before, here), 1, axis=1)
        return (east - west) * rows.half

    def north(here):
        return pltpu.roll(here, ROWS - 1, axis=0)

    def south(here):
        return pltpu.roll(here, 1, axis=0)

    def x(p, g):
        return x_ref[p, pl.ds(g * ROWS, ROWS), :]

    def around(p):
        return lax.rem(p + blocks - 1, blocks), lax.rem(p + 1, blocks)

    damping_north = [south(v) for v in damping]
    damping_south = [north(v) for v in damping]

    def first_pass(p, carry):
        before, after = around(p)
        for level in range(2):
            h, u, v = level, 2 + level, 4 + level
            thick, zonal = COURANT * x(p, h), x(p, u)
            div = zonal_diff(x(before, u), zonal, x(after, u))
            div = div + up * north(x(p, v)) - down * south(x(p, v))
            mix_ref[p, level] = damping[level] * div - thick
            rise = half_up * north(damping_north[level] * div - thick)
            rise = rise - half_down * south(damping_south[level] * div - thick)
            inc_ref[tile(p, v), :] = rise - COURANT * (rows.coriolis * zonal)
        return carry

    lax.fori_loop(0, blocks, first_pass, 0, unroll=blocks)

    def second_pass(p, carry):
        before, after = around(p)
        for level in range(2):
            h, u, v, t = level, 2 + level, 4 + level, 6 + level
            zonal, merid, potential = x(p, u), x(p, v), x(p, t)
            carried = 1.0 + x(p, h)
            flux_b, flux_a = (1.0 + x(before, h)) * x(before, u), (1.0 + x(after, h)) * x(after, u)
            flow = carried * merid
            inc_ref[tile(p, h), :] = -COURANT * (
                zonal_diff(flux_b, carried * zonal, flux_a) + up * north(flow) - down * south(flow)
            )
            inc_ref[tile(p, u), :] = COURANT * (rows.coriolis * merid) + zonal_diff(
                mix_ref[before, level], mix_ref[p, level], mix_ref[after, level]
            )
            rise = half_up * north(potential) - half_down * south(potential)
            inc_ref[tile(p, t), :] = -COURANT * (
                zonal * zonal_diff(x(before, t), potential, x(after, t)) + merid * rise
            )
        return carry

    lax.fori_loop(0, blocks, second_pass, 0, unroll=blocks)


def filter_kernel(
    bands,
    blocks,
    x_ref,
    inc_ref,
    z_ref,
    c_ref,
    own_ref,
    param_ref,
    twist_ref,
    forward_ref,
    inverse_ref,
    out_ref,
    more_ref,
    wave_ref,
):
    rows = Rows(bands)
    damping = [rows.square * param_ref[i] for i in range(2)]
    for side in range(2):
        edge, inner = side * (ROWS - 1), 1 + side * (ROWS - 3)
        across, inside = rows.beside(side)
        weight = rows.up[edge : edge + 1] if side else -rows.down[edge : edge + 1]
        step = 0.5 if side else -0.5
        for level in range(2):
            damp = damping[level]
            damp_edge, damp_inner = damp[edge : edge + 1], damp[inner : inner + 1]

            def beyond(k):
                other = c_ref[1 - rows.core, k * 2 + level]
                return jnp.where(rows.core == side, z_ref[k * 2 + level], other) * inside

            thick, near, potential, div = (beyond(k) for k in range(4))
            own = own_ref[side * 2 + level]
            div = div + across * own
            extra = weight * near
            more_ref[side, level] = -COURANT * weight * ((1.0 + thick) * near)
            more_ref[side, 2 + level] = damp_edge * rows.half[edge : edge + 1] * shifted_diff(extra)
            more_ref[side, 4 + level] = step * (damp_edge * div - COURANT * thick)
            more_ref[side, 6 + level] = -COURANT * step * (own * potential)
            more_ref[side, 8 + level] = step * damp_inner * extra

    row = lax.broadcasted_iota(jnp.int32, (ROWS, LANES), 0)
    order = way_back(blocks)

    def increment(p, g):
        def more(side, k):
            return more_ref[side, k, p : p + 1, :]

        total = jnp.where(row == 0, more(0, g), jnp.where(row == ROWS - 1, more(1, g), 0.0))
        if g // 2 == 2:
            total = jnp.where(row == 1, more(0, g + 4), total)
            total = jnp.where(row == ROWS - 2, more(1, g + 4), total)
        return inc_ref[tile(p, g), :] + total

    limit = param_ref[2].astype(jnp.int32)
    any_polar = (rows.first < rows.nlat // 4) | (rows.first + ROWS > rows.nlat - rows.nlat // 4)
    whole = rows.nlat // 4 % ROWS == 0
    top = blocks // 2
    nlon = blocks * LANES

    @pl.when(jnp.logical_not(any_polar))
    def _():
        for g in range(8):
            for p in range(blocks):
                out_ref[tile(order.index(p), g), :] = x_ref[tile(p, g), :] + increment(p, g)

    @pl.when(any_polar)
    def _():
        width = 2

        def analyse(part):
            for i in range(width):
                waves = real_fft([Signed(increment(p, part * width + i)) for p in range(blocks)])
                at = slice(i * ROWS, (i + 1) * ROWS)
                for k, (re, im) in enumerate(waves):
                    c, s = twist_ref[0, k], twist_ref[1, k]
                    if k == 0:
                        turned = re, Signed(jnp.zeros_like(re.value))
                    elif im is None:
                        turned = re * c, -(re * s)
                    else:
                        turned = re * c + im * s, im * c - re * s
                    wave_ref[part, k, at, :LANES] = turned[0].plain()
                    wave_ref[part, k, at, LANES:] = turned[1].plain()

        def product(values, table_ref):
            high, low = split(values)
            dot = lambda a, b: jnp.dot(a, b, preferred_element_type=jnp.float32)
            return dot(low, table_ref[0]) + dot(high, table_ref[0]) + dot(high, table_ref[1])

        wave = lax.broadcasted_iota(jnp.int32, (top + 1, 1, ROWS, LANES), 0)
        wave = wave + blocks * lax.broadcasted_iota(jnp.int32, (top + 1, 1, ROWS, LANES), 3)
        kept = jnp.minimum(wave, nlon - wave) <= limit
        kept = jnp.concatenate([kept, kept], axis=-1)

        def middle(part):
            count = (top + 1) * width * ROWS
            spectrum = product(wave_ref[part].reshape(count, 2 * LANES), forward_ref)
            spectrum = spectrum.reshape(top + 1, width, ROWS, 2 * LANES)
            spectrum = jnp.where(kept, spectrum, 0.0).reshape(count, 2 * LANES)
            smooth = product(spectrum, inverse_ref)
            wave_ref[part] = smooth.reshape(top + 1, width * ROWS, 2 * LANES)

        def rebuild(part):
            for i in range(width):
                g = part * width + i
                at = slice(i * ROWS, (i + 1) * ROWS)
                waves = []
                for k in range(top + 1):
                    re, im = (
                        Signed(wave_ref[part, k, at, j : j + LANES]) for j in (0, LANES)
                    )
                    c, s = twist_ref[0, k], twist_ref[1, k]
                    if k == 0:
                        waves.append((re, None))
                    elif k == top:
                        waves.append((re * c - im * s, None))
                    else:
                        waves.append((re * c - im * s, im * c + re * s))
                for p, smooth in enumerate(real_ifft(waves)):
                    smooth = smooth.plain()
                    if not whole:
                        smooth = jnp.where(rows.polar, smooth, increment(p, g))
                    out_ref[tile(order.index(p), g), :] = x_ref[tile(p, g), :] + smooth

        parts = 8 // width
        for i in range(parts + 2):
            if i < parts:
                analyse(i)
            if 1 <= i <= parts:
                middle(i - 1)
            if i >= 2:
                rebuild(i - 2)


def on_device(state, damping, cutoff):
    fields, levels, nrow, ncol = state.shape
    bands, blocks = lax.axis_size("lat"), lax.axis_size("lon")
    chips = blocks // 2
    vmem, hbm = pl.BlockSpec(memory_space=pltpu.VMEM), pl.BlockSpec(memory_space=pltpu.HBM)
    limits = pltpu.CompilerParams(vmem_limit_bytes=40 * 2**20)

    def call(kernel, name, out, ins, outs, cost, scratch=()):
        return pl.pallas_call(
            kernel,
            out_shape=out,
            in_specs=ins,
            out_specs=outs,
            scratch_shapes=scratch,
            compiler_params=limits,
            cost_estimate=pl.CostEstimate(flops=cost, bytes_accessed=2**22, transcendentals=0),
            name=name,
        )

    def array(*shape):
        return jax.ShapeDtypeStruct(shape, jnp.float32)

    parts = call(
        spread_kernel, "spread", array(chips, 2, fields, 2, ROWS, ncol), [vmem], vmem, 0
    )(state.reshape(fields, chips, 2, 2, ROWS, ncol))
    circles = lax.all_to_all(
        parts.reshape(blocks, -1, ncol), "lon", split_axis=0, concat_axis=0, tiled=True
    )

    twist, forward, inverse = fourier_tables(blocks)

    plane = array(8, blocks, ncol)
    z_mine = call(
        lambda *refs: pack_kernel(bands, *refs), "pack", plane, [vmem], vmem, 0
    )(circles)

    swaps = []
    for z in range(bands - 1):
        for m in range(chips):
            a, b = z * blocks + 2 * m + 1, (z + 1) * blocks + 2 * m
            swaps += [(a, b), (b, a)]
    z_other = lax.ppermute(z_mine, ("lat", "lon"), swaps)
    increments, params, c_mine, own = call(
        lambda *refs: stencil_kernel(bands, blocks, *refs),
        "stencil",
        (array(blocks * 8 * ROWS, ncol), array(3, ROWS, ncol), plane, array(4, blocks, ncol)),
        [vmem] * 3,
        (vmem,) * 4,
        2**28,
        [pltpu.VMEM((blocks, 2, ROWS, ncol), jnp.float32)],
    )(circles, damping, cutoff)
    pairs = [[2 * m, 2 * m + 1] for m in range(chips)]
    c_both = lax.all_gather(c_mine, "lon", axis_index_groups=pairs)
    moved = call(
        lambda *refs: filter_kernel(bands, blocks, *refs),
        "filter",
        array(blocks * 8 * ROWS, ncol),
        [vmem] * 9,
        vmem,
        2**31,
        [
            pltpu.VMEM((2, 10, blocks, ncol), jnp.float32),
            pltpu.VMEM((4, blocks // 2 + 1, 2 * ROWS, 2 * ncol), jnp.float32),
        ],
    )(circles.reshape(-1, ncol), increments, z_other, c_both, own, params, twist, forward, inverse)

    home = lax.all_to_all(
        moved.reshape(blocks, -1, ncol),
        "lon",
        split_axis=0,
        concat_axis=0,
        axis_index_groups=[way_back(blocks)],
        tiled=True,
    )
    whole = (fields, chips, 2, 2, ROWS, ncol)
    out = call(
        collect_kernel,
        "collect",
        array(*whole),
        [vmem],
        hbm,
        0,
        [pltpu.VMEM(whole, jnp.float32), pltpu.SemaphoreType.DMA((fields, 2))],
    )(home.reshape(blocks, fields, 2, ROWS, ncol))
    return out.reshape(state.shape)


def solution(mesh):
    in_specs = (P(None, None, "lat", "lon"), P(), P())
    out_specs = P(None, None, "lat", "lon")
    return jax.shard_map(
        on_device, mesh=mesh, in_specs=in_specs, out_specs=out_specs, check_vma=False
    )
```
